512 devices in a mesh: phase: 2 (over core), dp: 256 (over z, x, y).
Axes of the slice: x: 4, y: 4, z: 16, core: 2. Of those that a mesh axis runs over, the one named last changes fastest.
Arguments:
- tokens: bfloat16 [2, 24576, 1280], P(None, 'dp'), may hold values from -6 to 6
- segment_ids: int32 [2, 24576], replicated, may hold values from 0 to 3, as said below
- loss_mask: int32 [2, 24576], P(None, 'dp'), may hold values 0 or 1
- qkv_weight: bfloat16 [2, 1280, 3840], P('phase', 'dp'), may hold values from -0.15625 to 0.15625
- gains: float32 [2, 1280], P('phase'), may hold values from 0.5 to 1.5
- cotangent: bfloat16 [2, 24576, 1280], P(None, 'dp'), may hold values from -24 to 24
Outputs:
- boundary: bfloat16 [2, 2, 24576, 1280], P('phase', None, 'dp')
- gain_grad: float32 [2, 1280], P('phase', 'dp')
The draws below stay inside these ranges and needn't reach their ends.
Inputs may be any that keep to these rules, and one draw needn't show every extreme that they name: `segment_ids`: in each micro-batch the label is 0 at the first token and moves on by one, modulo 4, at the first token of each MSA sequence; it never changes elsewhere.
All inputs are finite; a program needn't handle non-finite values. No bound on the sum of `loss_mask` on one device may be relied on, other than what follows from the above.
Results may differ from the reference program's by a relative error of at most 0.014.
Values may be sent and summed in bfloat16 or wider, within the bound.
A program may use at most 128 MiB of HBM per device.

```python
import math
import jax
import jax.numpy as jnp
from jax import lax

WIDTH = 1280
HEADS = 16
HEAD_DIM = 80
MICRO = 2
TOK_DEV = 96
TOKENS = 24576


def draw_segment_ids(key, part):
    starts = jax.random.randint(jax.random.fold_in(key, 17), (MICRO, TOKENS), 0, 64) == 0
    overall = jnp.arange(TOKENS, dtype=jnp.int32)
    micro_rows = jnp.arange(MICRO, dtype=jnp.int32)
    forced = (micro_rows[:, None] == 0) & (overall[None, :] < 2 * TOK_DEV) & (overall[None, :] % (TOK_DEV // 2) == 0)
    starts = starts | (overall[None, :] == 0) | forced
    counted = jnp.cumsum(starts.astype(jnp.int32), axis=-1) - 1
    return (counted % 4).astype(jnp.int32)


def plant(values, rng, smallest, high):
    extent = values.shape
    place = [jax.random.randint(jax.random.fold_in(rng, axis), (), 0, extent[axis]) for axis in range(len(extent))]
    values = values.at[tuple(place)].set(smallest)
    longest = extent.index(max(extent))
    place[longest] = (place[longest] + 1) % extent[longest]
    return values.at[tuple(place)].set(high)


def strengthened(entries, stream_key, source, target, blocks, factor):
    def block_of(axis_at):
        return (jnp.arange(entries.shape[axis_at]) // (entries.shape[axis_at] // blocks)).reshape((-1,) + (1,) * (entries.ndim - 1 - axis_at))

    one_side = jax.random.permutation(stream_key, blocks)[block_of(target)]
    second = (block_of(target) + blocks // 2) % blocks
    return jnp.where((block_of(source) == one_side) | (block_of(source) == second), factor * entries, entries)


def shard_levels(rng, shape, pieces, least, largest):
    loudness = 1.0
    for axis_at, parts in pieces:
        heights = jax.random.uniform(jax.random.fold_in(jax.random.fold_in(rng, 6), axis_at), (parts,), jnp.float32, least / len(pieces), largest / len(pieces))
        loudness = loudness * jnp.repeat(jnp.exp(heights), shape[axis_at] // parts).reshape((-1,) + (1,) * (len(shape) - 1 - axis_at))
    return loudness


def centred(own_key, shape, spread, limit, shards=(), held_as=jnp.bfloat16):
    entries = jax.random.normal(own_key, shape, jnp.float32) * spread
    if len(shards) > 0:
        entries = shard_levels(own_key, shape, shards, -0.22, 0.18) * entries
    return jnp.clip(entries, min=-limit, max=limit).astype(held_as)


def gaussian_with(key, shape, spread, most, split, heavy, kind=jnp.bfloat16):
    values = spread * jax.random.normal(key, shape, jnp.float32)
    if split:
        values = values * shard_levels(key, shape, split, -0.22, 0.18)
    return jnp.clip(strengthened(values, jax.random.fold_in(key, 3), *heavy), -most, most).astype(kind)


def setup_inputs(seed: int = 0) -> dict:
    keys = jax.random.split(jax.random.key(seed), 7)
    return {
        "tokens": centred(keys[0], (MICRO, TOKENS, WIDTH), 1.0, 6.0, ((1, 256),)),
        "segment_ids": draw_segment_ids(jax.random.fold_in(keys[6], 71), 0),
        "loss_mask": plant((jax.random.randint(keys[2], (MICRO, TOKENS), 0, 3) < 1).astype(jnp.int32), jax.random.fold_in(keys[2], 1), 0, 1),
        "qkv_weight": centred(keys[3], (2, WIDTH, 3 * WIDTH), WIDTH ** -0.5, 0.15625, ((0, 2), (1, 256))),
        "gains": jnp.clip(1.0 + 0.1 * jax.random.normal(keys[4], (2, WIDTH), jnp.float32), 0.5, 1.5),
        "cotangent": gaussian_with(keys[5], (MICRO, TOKENS, WIDTH), 1.0, 24.0, ((1, 256),), (1, 2, 256, 6.0)),
    }


def normalize(inputs, scaling):
    widened = inputs.astype(jnp.float32)
    inverse = lax.rsqrt(lax.optimization_barrier(jnp.mean(widened * widened, axis=-1, keepdims=True)) + 1e-05)
    normed = (widened * inverse * scaling).astype(jnp.bfloat16)
    return (widened, inverse, normed)

def windows(project, labels):
    count = TOKENS // TOK_DEV
    shaped = project.reshape(count, TOK_DEV, 3, HEADS, HEAD_DIM)
    pairs = shaped[:, :, 1:]
    remote_pairs = jnp.concatenate([jnp.zeros_like(pairs[:1]), pairs[:-1]], axis=0)
    runs = labels.reshape(count, TOK_DEV)
    remote_runs = jnp.concatenate([runs[:1], runs[:-1]], axis=0)
    order = jnp.arange(count, dtype=jnp.int32)
    return (shaped, remote_pairs, runs, remote_runs, order)

def span_probs(shaped, remote_pairs, run_q, run_r, order):
    local = shaped.astype(jnp.float32)
    remote = remote_pairs.astype(jnp.float32)
    queries = local[:, 0]
    key_rows = jnp.concatenate([remote[:, 0], local[:, 1]], axis=0)
    values = jnp.concatenate([remote[:, 1], local[:, 2]], axis=0)
    position = jnp.arange(TOK_DEV)
    local_ok = (run_q[:, None] == run_q[None, :]) & (position[None, :] <= position[:, None])
    remote_ok = (run_q[:, None] == run_r[None, :]) & (order > 0)
    allowed = jnp.concatenate([remote_ok, local_ok], axis=1)
    scores = jnp.einsum('qhd,khd->hqk', queries, key_rows) / math.sqrt(HEAD_DIM)
    scores = jnp.where(allowed[None], scores, -1e+30)
    highest = lax.optimization_barrier(jnp.max(scores, axis=-1, keepdims=True))
    exponent = jnp.exp(scores - highest)
    softmax = exponent / lax.optimization_barrier(jnp.sum(exponent, axis=-1, keepdims=True))
    return (queries, key_rows, values, softmax)

def section_forward(inputs, labels, scaling, weight):
    widened, inverse, normed = normalize(inputs, scaling)
    project = jnp.dot(normed, weight, preferred_element_type=jnp.float32).astype(jnp.bfloat16)

    def one_run(group):
        queries, key_rows, values, softmax = span_probs(*group)
        rounded = lax.optimization_barrier(softmax.astype(jnp.bfloat16)).astype(jnp.float32)
        return jnp.einsum('hqk,khd->qhd', rounded, values).reshape(TOK_DEV, WIDTH)
    attended = lax.map(one_run, windows(project, labels)).reshape(TOKENS, WIDTH)
    return (widened + attended).astype(jnp.bfloat16)

def section_backward(inputs, labels, scaling, weight, upstream):
    widened, inverse, normed = normalize(inputs, scaling)
    project = jnp.dot(normed, weight, preferred_element_type=jnp.float32).astype(jnp.bfloat16)
    flowing = upstream.astype(jnp.float32)
    count = TOKENS // TOK_DEV
    shaped, remote_pairs, runs, remote_runs, order = windows(project, labels)
    flows = flowing.reshape(count, TOK_DEV, HEADS, HEAD_DIM)

    def one_run(group):
        queries, key_rows, values, softmax = span_probs(*group[:5])
        per_head = group[5]
        rounded = lax.optimization_barrier(softmax.astype(jnp.bfloat16)).astype(jnp.float32)
        grad_soft = jnp.einsum('qhd,khd->hqk', per_head, values)
        grad_values = jnp.einsum('hqk,qhd->khd', rounded, per_head)
        grad_scores = softmax * (grad_soft - lax.optimization_barrier(jnp.sum(softmax * grad_soft, axis=-1, keepdims=True))) / math.sqrt(HEAD_DIM)
        grad_queries = jnp.einsum('hqk,khd->qhd', grad_scores, key_rows)
        grad_keys = jnp.einsum('hqk,qhd->khd', grad_scores, queries)
        return (grad_queries.reshape(TOK_DEV, WIDTH), grad_keys.reshape(2 * TOK_DEV, WIDTH), grad_values.reshape(2 * TOK_DEV, WIDTH))
    grad_q, grad_k, grad_v = lax.map(one_run, (shaped, remote_pairs, runs, remote_runs, order, flows))
    zero_run = jnp.zeros((1, TOK_DEV, WIDTH), jnp.float32)
    own_k = grad_k[:, TOK_DEV:] + jnp.concatenate([grad_k[1:, :TOK_DEV], zero_run], axis=0)
    own_v = grad_v[:, TOK_DEV:] + jnp.concatenate([grad_v[1:, :TOK_DEV], zero_run], axis=0)
    grad_project = jnp.concatenate([grad_q.reshape(TOKENS, WIDTH), own_k.reshape(TOKENS, WIDTH), own_v.reshape(TOKENS, WIDTH)], axis=1).astype(jnp.bfloat16)
    grad_normed = jnp.dot(grad_project, weight.T, preferred_element_type=jnp.float32)
    grad_gain = lax.optimization_barrier(jnp.sum(grad_normed * widened * inverse, axis=0))
    scaled = grad_normed * scaling
    grad_inputs = inverse * (scaled - widened * inverse * inverse * lax.optimization_barrier(jnp.mean(scaled * widened, axis=-1, keepdims=True)))
    return ((flowing + grad_inputs).astype(jnp.bfloat16), grad_gain)

def reference(tokens, segment_ids, loss_mask, qkv_weight, gains, cotangent):
    outputs = []
    gradients = []
    first_total = jnp.zeros((WIDTH,), jnp.float32)
    second_total = jnp.zeros((WIDTH,), jnp.float32)
    for micro_index in range(MICRO):
        entering = tokens[micro_index]
        labels = segment_ids[micro_index]
        middle = section_forward(entering, labels, gains[0], qkv_weight[0])
        final = section_forward(middle, labels, gains[1], qkv_weight[1])
        selected = loss_mask[micro_index][:, None] == 1
        upstream = jnp.where(selected, cotangent[micro_index], jnp.zeros((), jnp.bfloat16))
        back_middle, gain_second = section_backward(middle, labels, gains[1], qkv_weight[1], upstream)
        back_first, gain_first = section_backward(entering, labels, gains[0], qkv_weight[0], back_middle)
        outputs.append(final)
        gradients.append(back_first)
        first_total = first_total + gain_first
        second_total = second_total + gain_second
    boundary = jnp.stack([jnp.stack(gradients), jnp.stack(outputs)])
    return (boundary, jnp.stack([first_total, second_total]))
```

```python
import functools
import math

import jax
import jax.numpy as jnp
from jax import lax
from jax.experimental import pallas as pl
from jax.experimental.pallas import tpu as pltpu
from jax.sharding import PartitionSpec as P

WIDTH = 1280
HEADS = 16
HEAD_DIM = 80
RUN = 96
PLANE = 16
LAYERS = 16
SIDE = 4
PANEL = 80
TILE = 128
HALF = 640
MESH = pl.DeviceIdType.MESH


def place():
    core = lax.axis_index("phase")
    dp = lax.axis_index("dp")
    z = dp // PLANE
    slot = dp % PLANE
    return core, dp, z, slot, slot // SIDE, slot % SIDE


def greet_plane_and_line(core, z, slot, line):
    barrier = pltpu.get_barrier_semaphore()
    mine = 2 * slot + core

    def plane(j, _):
        @pl.when(j != mine)
        def _():
            pl.semaphore_signal(barrier, inc=1, device_id=(j % 2, PLANE * z + j // 2), device_id_type=MESH)

    lax.fori_loop(0, 2 * PLANE, plane, None)
    if line == "neighbours":
        for step in (1, LAYERS - 1):
            pl.semaphore_signal(
                barrier, inc=1, device_id=(core, PLANE * ((z + step) % LAYERS) + slot), device_id_type=MESH
            )
        pl.semaphore_wait(barrier, 2 * PLANE - 1 + 2)
    else:

        def along(step, _):
            pl.semaphore_signal(
                barrier, inc=1, device_id=(core, PLANE * ((z + step) % LAYERS) + slot), device_id_type=MESH
            )

        lax.fori_loop(1, LAYERS, along, None)
        pl.semaphore_wait(barrier, 2 * PLANE - 1 + LAYERS - 1)


def gather_body(raw, w, sendbuf, stage, psend, pown, precv, zsend, zrecv, rsend, rrecv, ssend, srecv):
    core, dp, z, slot, x, y = place()
    greet_plane_and_line(core, z, slot, "neighbours")
    for c in range(2):
        for n in range(SIDE):
            sendbuf[c, n, :, :TILE] = raw[:, (5 * c + n) * TILE : (5 * c + n + 1) * TILE]
            sendbuf[c, n, :, TILE:] = raw[:, (5 * c + 4) * TILE : (5 * c + 5) * TILE]
    mine = 2 * slot + core

    def piece(j):
        c = j % 2
        i = j // 2
        n = jnp.where(c == 0, i % SIDE, i // SIDE)
        return pltpu.make_async_remote_copy(
            src_ref=sendbuf.at[c, n],
            dst_ref=stage.at[core, slot],
            send_sem=psend.at[j],
            recv_sem=precv.at[core],
            device_id=(c, PLANE * z + i),
            device_id_type=MESH,
        )

    ring_place = jnp.where(core == 0, y, x)
    own_piece = pltpu.make_async_copy(sendbuf.at[core, ring_place], stage.at[core, slot], precv.at[core])
    own_piece.start()

    def send_piece(j, _):
        @pl.when(j != mine)
        def _():
            piece(j).start()

    lax.fori_loop(0, 2 * PLANE, send_piece, None)
    base = 5 * core
    my_tile = base + ring_place
    row = lax.broadcasted_iota(jnp.int32, (3 * PANEL, 16 * PLANE), 0)
    column = lax.broadcasted_iota(jnp.int32, (3 * PANEL, 16 * PLANE), 1)
    within = row % PANEL
    wanted = (within // 5) * 16 + (row // PANEL) * 5 + within % 5
    select = (column == wanted).astype(jnp.float32).astype(jnp.bfloat16)
    rows = pl.ds(pl.multiple_of(PANEL * z, 16), PANEL)
    for s in range(2):
        pltpu.make_async_copy(stage.at[s], stage.at[s], precv.at[s]).wait()
        panel = jnp.dot(
            select, stage[s].reshape(16 * PLANE, 2 * TILE), preferred_element_type=jnp.float32
        ).astype(jnp.bfloat16)
        for t in range(3):
            w[s, t, rows, pl.ds(pl.multiple_of(TILE * my_tile, TILE), TILE)] = panel[
                t * PANEL : (t + 1) * PANEL, :TILE
            ]
            w[s, t, rows, pl.ds(pl.multiple_of(TILE * (base + 4), TILE), TILE)] = panel[
                t * PANEL : (t + 1) * PANEL, TILE:
            ]

    def drain_piece(j, _):
        @pl.when(j != mine)
        def _():
            piece(j).wait_send()

    lax.fori_loop(0, 2 * PLANE, drain_piece, None)

    def region(s, panel, tile, width=TILE):
        return w.at[
            s,
            :,
            pl.ds(pl.multiple_of(PANEL * panel, 16), PANEL),
            pl.ds(pl.multiple_of(TILE * tile, TILE), width),
        ]

    def tile_of(kind):
        return my_tile if kind == 0 else base + 4

    def panel_of(q):
        k = (q + 1) // 2
        sign = jnp.where(q % 2 == 1, -1, 1)
        return (z + sign * k + LAYERS) % LAYERS

    def z_copy(s, kind, panel, upward):
        to = (z + jnp.where(upward == 1, 1, LAYERS - 1)) % LAYERS
        piece_ref = region(s, panel, tile_of(kind))
        return pltpu.make_async_remote_copy(
            src_ref=piece_ref,
            dst_ref=piece_ref,
            send_sem=zsend.at[s, kind, upward, panel],
            recv_sem=zrecv.at[s, kind, panel],
            device_id=(core, PLANE * to + slot),
            device_id_type=MESH,
        )

    def ring_device(step):
        moved = (ring_place + step) % SIDE
        return PLANE * z + jnp.where(core == 0, SIDE * x + moved, SIDE * moved + y)

    def ring_tile(step):
        return base + (ring_place + step) % SIDE

    def ring_copy(s, panel, tile, step, way):
        piece_ref = region(s, panel, tile)
        return pltpu.make_async_remote_copy(
            src_ref=piece_ref,
            dst_ref=piece_ref,
            send_sem=rsend.at[s, panel, way],
            recv_sem=rrecv.at[s, panel, way],
            device_id=(core, ring_device(step)),
            device_id_type=MESH,
        )

    def passed_on(s, panel):
        even = panel % 2 == 0
        tile = jnp.where(even, ring_tile(SIDE - 1), ring_tile(1))
        return ring_copy(s, panel, tile, jnp.where(even, 1, SIDE - 1), 2)

    def sibling_copy(s, panel):
        piece_ref = region(s, panel, base, HALF)
        return pltpu.make_async_remote_copy(
            src_ref=piece_ref,
            dst_ref=piece_ref,
            send_sem=ssend.at[s, panel],
            recv_sem=srecv.at[s, panel],
            device_id=(1 - core, dp),
            device_id_type=MESH,
        )

    def step(i, _):
        @pl.when(i < 32)
        def _():
            s, q = i // 16, i % 16
            panel = panel_of(q)
            upward = q % 2

            @pl.when(q == 0)
            def _():
                for kind in range(2):
                    for way in range(2):
                        z_copy(s, kind, panel, way).start()

            @pl.when(q > 0)
            def _():
                z_copy(s, 0, panel, upward).wait_recv()

                @pl.when(q < 14)
                def _():
                    z_copy(s, 0, panel, upward).start()

                z_copy(s, 1, panel, upward).wait_recv()

                @pl.when((q < 13) | (q == 14))
                def _():
                    z_copy(s, 1, panel, upward).start()

            ring_copy(s, panel, my_tile, 1, 0).start()
            ring_copy(s, panel, my_tile, SIDE - 1, 1).start()

        @pl.when((i >= 1) & (i < 33))
        def _():
            s, q = (i - 1) // 16, (i - 1) % 16
            panel = panel_of(q)
            ring_copy(s, panel, ring_tile(SIDE - 1), 1, 0).wait_recv()
            ring_copy(s, panel, ring_tile(1), 1, 1).wait_recv()
            passed_on(s, panel).start()

        @pl.when(i >= 2)
        def _():
            s, q = (i - 2) // 16, (i - 2) % 16
            panel = panel_of(q)
            ring_copy(s, panel, ring_tile(2), 1, 2).wait_recv()
            sibling_copy(s, panel).start()

    lax.fori_loop(0, 34, step, None)

    def finish(i, _):
        s, q = i // 16, i % 16
        panel = panel_of(q)
        sibling_copy(s, panel).wait()

        for way in range(3):
            ring_copy(s, panel, my_tile, 1, way).wait_send()

        @pl.when(q == 0)
        def _():
            for kind in range(2):
                for way in range(2):
                    z_copy(s, kind, panel, way).wait_send()

        @pl.when((q > 0) & (q < 14))
        def _():
            z_copy(s, 0, panel, q % 2).wait_send()

        @pl.when(((q > 0) & (q < 13)) | (q == 14))
        def _():
            z_copy(s, 1, panel, q % 2).wait_send()

    lax.fori_loop(0, 32, finish, None)


GATHER_SCRATCH = [
    pltpu.VMEM((2, SIDE, 16, 2 * TILE), jnp.bfloat16),
    pltpu.VMEM((2, PLANE, 16, 2 * TILE), jnp.bfloat16),
    pltpu.SemaphoreType.DMA((2 * PLANE,)),
    pltpu.SemaphoreType.DMA,
    pltpu.SemaphoreType.DMA((2,)),
    pltpu.SemaphoreType.DMA((2, 2, 2, LAYERS)),
    pltpu.SemaphoreType.DMA((2, 2, LAYERS)),
    pltpu.SemaphoreType.DMA((2, LAYERS, 3)),
    pltpu.SemaphoreType.DMA((2, LAYERS, 3)),
    pltpu.SemaphoreType.DMA((2, LAYERS)),
    pltpu.SemaphoreType.DMA((2, LAYERS)),
]


def gather_kernel(raw, out, w, outsem, *scratch):
    gather_body(raw, w, *scratch)
    copy = pltpu.make_async_copy(w, out, outsem)
    copy.start()
    copy.wait()


def gathered(shard):
    raw = jnp.transpose(shard.reshape(5, 3, WIDTH), (1, 0, 2)).reshape(15, WIDTH)
    raw = jnp.pad(raw, ((0, 1), (0, 0)))
    return pl.pallas_call(
        gather_kernel,
        out_shape=jax.ShapeDtypeStruct((2, 3, WIDTH, WIDTH), jnp.bfloat16),
        in_specs=[pl.BlockSpec(memory_space=pltpu.VMEM)],
        out_specs=pl.BlockSpec(memory_space=pl.ANY),
        scratch_shapes=[pltpu.VMEM((2, 3, WIDTH, WIDTH), jnp.bfloat16), pltpu.SemaphoreType.DMA]
        + GATHER_SCRATCH,
        compiler_params=pltpu.CompilerParams(
            collective_id=0, has_side_effects=True, vmem_limit_bytes=48 * 2**20
        ),
        name="gather",
    )(raw)


def reduce_kernel(terms, out, part, line, both, plane, lsend, lrecv, psend, precv):
    core, dp, z, slot, x, y = place()
    greet_plane_and_line(core, z, slot, "line")
    for k in range(LAYERS):
        part[k, 0:2, :] = jnp.concatenate(
            [terms[:, PANEL * k : PANEL * (k + 1)], jnp.zeros((2, TILE - PANEL), jnp.float32)], axis=1
        )

    def along(step):
        to = (z + step) % LAYERS
        return pltpu.make_async_remote_copy(
            src_ref=part.at[to],
            dst_ref=line.at[step],
            send_sem=lsend.at[step],
            recv_sem=lrecv.at[step],
            device_id=(core, PLANE * to + slot),
            device_id_type=MESH,
        )

    def start_along(step, _):
        along(step).start()

    lax.fori_loop(1, LAYERS, start_along, None)
    total = part[z, 0:2, :]
    for step in range(1, LAYERS):
        along(step).wait_recv()
        total = total + line[step, 0:2, :]
    both[0] = jnp.broadcast_to(total[0:1], (8, TILE))
    both[1] = jnp.broadcast_to(total[1:2], (8, TILE))
    mine = 2 * slot + core

    def across(j):
        return pltpu.make_async_remote_copy(
            src_ref=both.at[j % 2],
            dst_ref=plane.at[mine],
            send_sem=psend.at[j],
            recv_sem=precv.at[mine],
            device_id=(j % 2, PLANE * z + j // 2),
            device_id_type=MESH,
        )

    def start_across(j, _):
        @pl.when(j != mine)
        def _():
            across(j).start()

    lax.fori_loop(0, 2 * PLANE, start_across, None)
    plane[mine] = both[core]

    def arrive(j, _):
        @pl.when(j != mine)
        def _():
            pltpu.make_async_copy(plane.at[j], plane.at[j], precv.at[j]).wait()

    lax.fori_loop(0, 2 * PLANE, arrive, None)
    out[...] = jnp.sum(plane[...], axis=0)[0:1]

    def drain_along(step, _):
        along(step).wait_send()

    lax.fori_loop(1, LAYERS, drain_along, None)

    def drain_across(j, _):
        @pl.when(j != mine)
        def _():
            across(j).wait_send()

    lax.fori_loop(0, 2 * PLANE, drain_across, None)


def reduced(terms):
    row = pl.pallas_call(
        reduce_kernel,
        out_shape=jax.ShapeDtypeStruct((1, TILE), jnp.float32),
        in_specs=[pl.BlockSpec(memory_space=pltpu.VMEM)],
        out_specs=pl.BlockSpec(memory_space=pltpu.VMEM),
        scratch_shapes=[
            pltpu.VMEM((LAYERS, 8, TILE), jnp.float32),
            pltpu.VMEM((LAYERS, 8, TILE), jnp.float32),
            pltpu.VMEM((2, 8, TILE), jnp.float32),
            pltpu.VMEM((2 * PLANE, 8, TILE), jnp.float32),
            pltpu.SemaphoreType.DMA((LAYERS,)),
            pltpu.SemaphoreType.DMA((LAYERS,)),
            pltpu.SemaphoreType.DMA((2 * PLANE,)),
            pltpu.SemaphoreType.DMA((2 * PLANE,)),
        ],
        compiler_params=pltpu.CompilerParams(collective_id=1, has_side_effects=True),
        name="reduce",
    )(terms)
    slot = lax.axis_index("dp") % PLANE
    return lax.dynamic_slice(row, (0, 5 * slot), (1, 5))


def passed_along(x, axis, by):
    size = lax.axis_size(axis)
    pairs = [(i, i + by) for i in range(size) if 0 <= i + by < size]
    return lax.ppermute(x, axis, pairs)


def heads_of(x):
    return x.reshape(x.shape[0], HEADS, HEAD_DIM).astype(jnp.float32)


def forward(x, w, scaling, allowed):
    widened = x.astype(jnp.float32)
    inverse = lax.rsqrt(jnp.mean(widened * widened, axis=-1, keepdims=True) + 1e-05)
    normed = (widened * inverse * scaling).astype(jnp.bfloat16)
    q, k, v = (jnp.dot(normed, w[t], preferred_element_type=jnp.float32).astype(jnp.bfloat16) for t in range(3))
    remote = passed_along(jnp.concatenate([k, v], axis=1), "dp", 1)
    queries = heads_of(q)
    keys = heads_of(jnp.concatenate([remote[:, :WIDTH], k], axis=0))
    values = heads_of(jnp.concatenate([remote[:, WIDTH:], v], axis=0))
    scores = jnp.einsum("qhd,khd->hqk", queries, keys) / math.sqrt(HEAD_DIM)
    scores = jnp.where(allowed[None], scores, -1e30)
    exponent = jnp.exp(scores - jnp.max(scores, axis=-1, keepdims=True))
    softmax = exponent / jnp.sum(exponent, axis=-1, keepdims=True)
    rounded = softmax.astype(jnp.bfloat16).astype(jnp.float32)
    attended = jnp.einsum("hqk,khd->qhd", rounded, values)
    out = (widened + attended.reshape(RUN, WIDTH)).astype(jnp.bfloat16)
    return out, (widened, inverse, queries, keys, values, softmax, rounded)


def backward(record, w, scaling, upstream):
    widened, inverse, queries, keys, values, softmax, rounded = record
    flowing = upstream.astype(jnp.float32)
    per_head = heads_of(upstream)
    grad_soft = jnp.einsum("qhd,khd->hqk", per_head, values)
    grad_values = jnp.einsum("hqk,qhd->khd", rounded, per_head)
    grad_scores = (
        softmax * (grad_soft - jnp.sum(softmax * grad_soft, axis=-1, keepdims=True)) / math.sqrt(HEAD_DIM)
    )
    grad_q = jnp.einsum("hqk,khd->qhd", grad_scores, keys).reshape(RUN, WIDTH)
    grad_k = jnp.einsum("hqk,qhd->khd", grad_scores, queries).reshape(2 * RUN, WIDTH)
    grad_v = grad_values.reshape(2 * RUN, WIDTH)
    away = jnp.concatenate([grad_k[:RUN], grad_v[:RUN]], axis=1).astype(jnp.bfloat16)
    back = passed_along(away, "dp", -1).astype(jnp.float32)
    grads = (grad_q, grad_k[RUN:] + back[:, :WIDTH], grad_v[RUN:] + back[:, WIDTH:])
    grad_normed = sum(
        lax.dot_general(g.astype(jnp.bfloat16), w[t], (((1,), (1,)), ((), ())), preferred_element_type=jnp.float32)
        for t, g in enumerate(grads)
    )
    gain = jnp.sum(grad_normed * widened * inverse, axis=0)
    scaled = grad_normed * scaling
    grad_in = inverse * (scaled - widened * inverse * inverse * jnp.mean(scaled * widened, axis=-1, keepdims=True))
    return (flowing + grad_in).astype(jnp.bfloat16), gain


def shards(tokens, segment_ids, loss_mask, qkv_weight, gains, cotangent):
    core = lax.axis_index("phase")
    dp = lax.axis_index("dp")
    w = gathered(qkv_weight[0])
    other = lax.ppermute(gains, "phase", [(0, 1), (1, 0)])
    scale = jnp.where(core == 0, jnp.concatenate([gains, other]), jnp.concatenate([other, gains]))
    x = jnp.where(core == 0, tokens[0], tokens[1])
    seg = jnp.where(core == 0, segment_ids[0], segment_ids[1])
    seg_own = lax.dynamic_slice_in_dim(seg, dp * RUN, RUN)
    seg_prev = lax.dynamic_slice_in_dim(seg, jnp.maximum(dp - 1, 0) * RUN, RUN)
    position = jnp.arange(RUN)
    own_ok = (seg_own[:, None] == seg_own[None, :]) & (position[None, :] <= position[:, None])
    prev_ok = (seg_own[:, None] == seg_prev[None, :]) & (dp > 0)
    allowed = jnp.concatenate([prev_ok, own_ok], axis=1)
    middle, first = forward(x, w[0], scale[0], allowed)
    final, second = forward(middle, w[1], scale[1], allowed)
    cot = jnp.where(core == 0, cotangent[0], cotangent[1])
    mask = jnp.where(core == 0, loss_mask[0], loss_mask[1])
    upstream = jnp.where(mask[:, None] == 1, cot, jnp.zeros((), jnp.bfloat16))
    middle_grad, gain_second = backward(second, w[1], scale[1], upstream)
    grad, gain_first = backward(first, w[0], scale[0], middle_grad)
    handed = jnp.where(core == 0, final, grad)
    kept = jnp.where(core == 0, grad, final)
    got = lax.ppermute(handed, "phase", [(0, 1), (1, 0)])
    boundary = jnp.where(core == 0, jnp.stack([kept, got]), jnp.stack([got, kept]))[None]
    return boundary, reduced(jnp.stack([gain_first, gain_second]))


def solution(mesh):
    in_specs = (
        P(None, "dp", None),
        P(),
        P(None, "dp"),
        P("phase", "dp", None),
        P("phase", None),
        P(None, "dp", None),
    )
    out_specs = (P("phase", None, "dp", None), P("phase", "dp"))
    return jax.shard_map(shards, mesh=mesh, in_specs=in_specs, out_specs=out_specs, check_vma=False)
```

```python
import functools
import math

import jax
import jax.numpy as jnp
from jax import lax
from jax.experimental import pallas as pl
from jax.experimental.pallas import tpu as pltpu
from jax.sharding import PartitionSpec as P

WIDTH = 1280
HEADS = 16
HEAD_DIM = 80
RUN = 96
PLANE = 16
LAYERS = 16
SIDE = 4
PANEL = 80
TILE = 128
HALF = 640
RING_LAG = 4
CHIP_LAG = 8
DEVICES = 256
NEVER = -1e30
MESH = pl.DeviceIdType.MESH


def place():
    core = lax.axis_index("phase")
    dp = lax.axis_index("dp")
    z = dp // PLANE
    slot = dp % PLANE
    return core, dp, z, slot, slot // SIDE, slot % SIDE


def greet(core, dp, z, slot):
    barrier = pltpu.get_barrier_semaphore()
    mine = 2 * slot + core

    def plane(j, _):
        @pl.when(j != mine)
        def _():
            pl.semaphore_signal(barrier, inc=1, device_id=(j % 2, PLANE * z + j // 2), device_id_type=MESH)

    lax.fori_loop(0, 2 * PLANE, plane, None)

    def along(step, _):
        pl.semaphore_signal(
            barrier, inc=1, device_id=(core, PLANE * ((z + step) % LAYERS) + slot), device_id_type=MESH
        )

    lax.fori_loop(1, LAYERS, along, None)
    for step in (1, DEVICES - 1):
        pl.semaphore_signal(barrier, inc=1, device_id=(core, (dp + step) % DEVICES), device_id_type=MESH)
    pl.semaphore_wait(barrier, 2 * PLANE - 1 + LAYERS - 1 + 2)


def gather_body(raw, w, sendbuf, stage, psend, pown, precv, zsend, zrecv, rsend, rrecv, ssend, srecv):
    core, dp, z, slot, x, y = place()
    for c in range(2):
        for n in range(SIDE):
            sendbuf[c, n, :, :TILE] = raw[:, (5 * c + n) * TILE : (5 * c + n + 1) * TILE]
            sendbuf[c, n, :, TILE:] = raw[:, (5 * c + 4) * TILE : (5 * c + 5) * TILE]
    mine = 2 * slot + core

    def piece(j):
        c = j % 2
        i = j // 2
        n = jnp.where(c == 0, i % SIDE, i // SIDE)
        return pltpu.make_async_remote_copy(
            src_ref=sendbuf.at[c, n],
            dst_ref=stage.at[core, slot],
            send_sem=psend.at[j],
            recv_sem=precv.at[core],
            device_id=(c, PLANE * z + i),
            device_id_type=MESH,
        )

    ring_place = jnp.where(core == 0, y, x)
    own_piece = pltpu.make_async_copy(sendbuf.at[core, ring_place], stage.at[core, slot], precv.at[core])
    own_piece.start()

    def send_piece(j, _):
        @pl.when(j != mine)
        def _():
            piece(j).start()

    lax.fori_loop(0, 2 * PLANE, send_piece, None)
    base = 5 * core
    my_tile = base + ring_place
    row = lax.broadcasted_iota(jnp.int32, (3 * PANEL, 16 * PLANE), 0)
    column = lax.broadcasted_iota(jnp.int32, (3 * PANEL, 16 * PLANE), 1)
    within = row % PANEL
    wanted = (within // 5) * 16 + (row // PANEL) * 5 + within % 5
    select = (column == wanted).astype(jnp.float32).astype(jnp.bfloat16)
    rows = pl.ds(pl.multiple_of(PANEL * z, 16), PANEL)
    for s in range(2):
        pltpu.make_async_copy(stage.at[s], stage.at[s], precv.at[s]).wait()
        panel = jnp.dot(
            select, stage[s].reshape(16 * PLANE, 2 * TILE), preferred_element_type=jnp.float32
        ).astype(jnp.bfloat16)
        for t in range(3):
            w[s, t, rows, pl.ds(pl.multiple_of(TILE * my_tile, TILE), TILE)] = panel[
                t * PANEL : (t + 1) * PANEL, :TILE
            ]
            w[s, t, rows, pl.ds(pl.multiple_of(TILE * (base + 4), TILE), TILE)] = panel[
                t * PANEL : (t + 1) * PANEL, TILE:
            ]

    def drain_piece(j, _):
        @pl.when(j != mine)
        def _():
            piece(j).wait_send()

    lax.fori_loop(0, 2 * PLANE, drain_piece, None)

    def region(s, panel, tile, width=TILE):
        return w.at[
            s,
            :,
            pl.ds(pl.multiple_of(PANEL * panel, 16), PANEL),
            pl.ds(pl.multiple_of(TILE * tile, TILE), width),
        ]

    def tile_of(kind):
        return my_tile if kind == 0 else base + 4

    def panel_of(q):
        k = (q + 1) // 2
        sign = jnp.where(q % 2 == 1, -1, 1)
        return (z + sign * k + LAYERS) % LAYERS

    def z_copy(s, kind, panel, upward):
        to = (z + jnp.where(upward == 1, 1, LAYERS - 1)) % LAYERS
        piece_ref = region(s, panel, tile_of(kind))
        return pltpu.make_async_remote_copy(
            src_ref=piece_ref,
            dst_ref=piece_ref,
            send_sem=zsend.at[s, kind, upward, panel],
            recv_sem=zrecv.at[s, kind, panel],
            device_id=(core, PLANE * to + slot),
            device_id_type=MESH,
        )

    def ring_device(step):
        moved = (ring_place + step) % SIDE
        return PLANE * z + jnp.where(core == 0, SIDE * x + moved, SIDE * moved + y)

    def ring_tile(step):
        return base + (ring_place + step) % SIDE

    def ring_copy(s, panel, tile, step, way):
        piece_ref = region(s, panel, tile)
        return pltpu.make_async_remote_copy(
            src_ref=piece_ref,
            dst_ref=piece_ref,
            send_sem=rsend.at[s, panel, way],
            recv_sem=rrecv.at[s, panel, way],
            device_id=(core, ring_device(step)),
            device_id_type=MESH,
        )

    def passed_on(s, panel):
        even = panel % 2 == 0
        tile = jnp.where(even, ring_tile(SIDE - 1), ring_tile(1))
        return ring_copy(s, panel, tile, jnp.where(even, 1, SIDE - 1), 2)

    def sibling_copy(s, panel):
        piece_ref = region(s, panel, base, HALF)
        return pltpu.make_async_remote_copy(
            src_ref=piece_ref,
            dst_ref=piece_ref,
            send_sem=ssend.at[s, panel],
            recv_sem=srecv.at[s, panel],
            device_id=(1 - core, dp),
            device_id_type=MESH,
        )

    def step(i, _):
        @pl.when(i < 32)
        def _():
            s, q = i % 2, i // 2
            panel = panel_of(q)
            upward = q % 2

            @pl.when(q == 0)
            def _():
                for kind in range(2):
                    for way in range(2):
                        z_copy(s, kind, panel, way).start()

            @pl.when(q > 0)
            def _():
                z_copy(s, 0, panel, upward).wait_recv()

                @pl.when(q < 14)
                def _():
                    z_copy(s, 0, panel, upward).start()

                z_copy(s, 1, panel, upward).wait_recv()

                @pl.when((q < 13) | (q == 14))
                def _():
                    z_copy(s, 1, panel, upward).start()

            ring_copy(s, panel, my_tile, 1, 0).start()
            ring_copy(s, panel, my_tile, SIDE - 1, 1).start()

        @pl.when((i >= RING_LAG) & (i < 32 + RING_LAG))
        def _():
            s, q = (i - RING_LAG) % 2, (i - RING_LAG) // 2
            panel = panel_of(q)
            ring_copy(s, panel, ring_tile(SIDE - 1), 1, 0).wait_recv()
            ring_copy(s, panel, ring_tile(1), 1, 1).wait_recv()
            passed_on(s, panel).start()

        @pl.when(i >= CHIP_LAG)
        def _():
            s, q = (i - CHIP_LAG) % 2, (i - CHIP_LAG) // 2
            panel = panel_of(q)
            ring_copy(s, panel, ring_tile(2), 1, 2).wait_recv()
            sibling_copy(s, panel).start()

    lax.fori_loop(0, 32 + CHIP_LAG, step, None)

    def arrive(i, _):
        sibling_copy(i // 16, i % 16).wait_recv()

    lax.fori_loop(0, 32, arrive, None)

    def finish(i, _):
        s, q = i // 16, i % 16
        panel = panel_of(q)
        sibling_copy(s, panel).wait_send()

        for way in range(3):
            ring_copy(s, panel, my_tile, 1, way).wait_send()

        @pl.when(q == 0)
        def _():
            for kind in range(2):
                for way in range(2):
                    z_copy(s, kind, panel, way).wait_send()

        @pl.when((q > 0) & (q < 14))
        def _():
            z_copy(s, 0, panel, q % 2).wait_send()

        @pl.when(((q > 0) & (q < 13)) | (q == 14))
        def _():
            z_copy(s, 1, panel, q % 2).wait_send()

    return lambda: lax.fori_loop(0, 32, finish, None)


GATHER_SCRATCH = [
    pltpu.VMEM((2, SIDE, 16, 2 * TILE), jnp.bfloat16),
    pltpu.VMEM((2, PLANE, 16, 2 * TILE), jnp.bfloat16),
    pltpu.SemaphoreType.DMA((2 * PLANE,)),
    pltpu.SemaphoreType.DMA,
    pltpu.SemaphoreType.DMA((2,)),
    pltpu.SemaphoreType.DMA((2, 2, 2, LAYERS)),
    pltpu.SemaphoreType.DMA((2, 2, LAYERS)),
    pltpu.SemaphoreType.DMA((2, LAYERS, 3)),
    pltpu.SemaphoreType.DMA((2, LAYERS, 3)),
    pltpu.SemaphoreType.DMA((2, LAYERS)),
    pltpu.SemaphoreType.DMA((2, LAYERS)),
]


def reduce_body(terms, out, part, line, both, plane, lsend, lrecv, psend, precv):
    core, dp, z, slot, x, y = place()
    for k in range(LAYERS):
        part[k, 0:2, :] = jnp.concatenate(
            [terms[0:2, PANEL * k : PANEL * (k + 1)], jnp.zeros((2, TILE - PANEL), jnp.float32)], axis=1
        )

    def along(step):
        to = (z + step) % LAYERS
        return pltpu.make_async_remote_copy(
            src_ref=part.at[to],
            dst_ref=line.at[step],
            send_sem=lsend.at[step],
            recv_sem=lrecv.at[step],
            device_id=(core, PLANE * to + slot),
            device_id_type=MESH,
        )

    def start_along(step, _):
        along(step).start()

    lax.fori_loop(1, LAYERS, start_along, None)
    total = part[z, 0:2, :]
    for step in range(1, LAYERS):
        along(step).wait_recv()
        total = total + line[step, 0:2, :]
    both[0] = jnp.broadcast_to(total[0:1], (8, TILE))
    both[1] = jnp.broadcast_to(total[1:2], (8, TILE))
    mine = 2 * slot + core

    def across(j):
        return pltpu.make_async_remote_copy(
            src_ref=both.at[j % 2],
            dst_ref=plane.at[mine],
            send_sem=psend.at[j],
            recv_sem=precv.at[mine],
            device_id=(j % 2, PLANE * z + j // 2),
            device_id_type=MESH,
        )

    def start_across(j, _):
        @pl.when(j != mine)
        def _():
            across(j).start()

    lax.fori_loop(0, 2 * PLANE, start_across, None)
    plane[mine] = both[core]

    def arrive(j, _):
        @pl.when(j != mine)
        def _():
            pltpu.make_async_copy(plane.at[j], plane.at[j], precv.at[j]).wait()

    lax.fori_loop(0, 2 * PLANE, arrive, None)
    out[...] = jnp.sum(plane[...], axis=0)[0:1]

    def drain_along(step, _):
        along(step).wait_send()

    lax.fori_loop(1, LAYERS, drain_along, None)

    def drain_across(j, _):
        @pl.when(j != mine)
        def _():
            across(j).wait_send()

    lax.fori_loop(0, 2 * PLANE, drain_across, None)


def windows():
    for j in range(8):
        first = HEAD_DIM * j
        start = first // TILE * TILE
        stop = -(-(first + HEAD_DIM) // TILE) * TILE
        yield j, start, stop - start, first - start


def lanes(rows, width, offset):
    lane = lax.broadcasted_iota(jnp.int32, (rows, width), 1)
    return (lane >= offset) & (lane < offset + HEAD_DIM)


def nt(a, b):
    return lax.dot_general(a, b, (((1,), (1,)), ((), ())), preferred_element_type=jnp.float32)


def tn(a, b):
    return lax.dot_general(a, b, (((0,), (0,)), ((), ())), preferred_element_type=jnp.float32)


def nn(a, b):
    return jnp.dot(a, b, preferred_element_type=jnp.float32)


def each_group(body):
    lax.fori_loop(0, 2, lambda g, _: body(g, pl.multiple_of(HALF * g, TILE)), None)


def kept_lanes(ref, cols, value, keep):
    ref[:, cols] = jnp.where(keep, value, ref[:, cols])


def masked(value, keep):
    return jnp.where(keep, value, jnp.zeros((), value.dtype))


def project(s, r):
    x = r["x"][s].reshape(3 * RUN, WIDTH).astype(jnp.float32)
    inverse = lax.rsqrt(jnp.mean(x * x, axis=-1, keepdims=True) + 1e-05)
    r["normed"][...] = (x * inverse * r["scale"][s]).astype(jnp.bfloat16)
    r["inverse"][s] = jnp.broadcast_to(inverse[RUN : 2 * RUN], (RUN, TILE))
    for t, first in ((0, RUN), (1, 0), (2, 0)):

        def chunk(n, _):
            cols = pl.ds(pl.multiple_of(256 * n, 256), 256)
            r["qkv"][s, t, :, cols] = nn(r["normed"][first : first + 2 * RUN], r["w"][s, t, :, cols]).astype(
                jnp.bfloat16
            )

        lax.fori_loop(0, 5, chunk, None)


def attend(s, r):
    att = r["acc"].at[0]

    def group(g, base):
        for j, start, width, offset in windows():
            cols = pl.ds(base + start, width)
            keep = lanes(RUN, width, offset)
            query = masked(r["qkv"][s, 0, :RUN, cols], keep)
            scores = nt(r["qkv"][s, 1, :, cols], query) * (1.0 / math.sqrt(HEAD_DIM)) + r["bias"][...]
            highest = jnp.max(scores, axis=0, keepdims=True)
            exponent = jnp.exp(scores - highest)
            total = jnp.sum(exponent, axis=0, keepdims=True)
            soft = exponent / total
            r["soft"][s, 8 * g + j] = soft
            r["stats"][s, 8 * g + j, :, :RUN] = highest + jnp.log(total)
            kept_lanes(att, cols, tn(soft.astype(jnp.bfloat16), r["qkv"][s, 2, :, cols]), keep)

    each_group(group)
    return (r["x"][s, 1].astype(jnp.float32) + att[...]).astype(jnp.bfloat16)


def score_grads(s, r):
    def group(g, base):
        for j, start, width, offset in windows():
            cols = pl.ds(base + start, width)
            h = 8 * g + j
            flow = masked(r["flow"][s, 0, :, cols], lanes(RUN, width, offset))
            grad_soft = nt(r["qkv"][s, 2, :, cols], flow)
            soft = r["soft"][s, h]
            inner = jnp.sum(soft * grad_soft, axis=0, keepdims=True)
            r["stats"][2 + s, h, :, :RUN] = inner
            grad = (soft * (grad_soft - inner) * (1.0 / math.sqrt(HEAD_DIM))).astype(jnp.bfloat16)
            r["ds"][h] = grad
            r["softb"][h, :, :RUN] = soft[RUN:].astype(jnp.bfloat16)

    each_group(group)


def query_grads(s, r):
    def group(g, base):
        for j, start, width, offset in windows():
            cols = pl.ds(base + start, width)
            keep = lanes(RUN, width, offset)
            kept_lanes(r["acc"].at[0], cols, tn(r["ds"][8 * g + j], r["qkv"][s, 1, :, cols]), keep)

    each_group(group)
    r["gqkv"][0] = r["acc"][0].astype(jnp.bfloat16)


def next_soft(s, r):
    def group(g, base):
        for j, start, width, offset in windows():
            cols = pl.ds(base + start, width)
            query = masked(r["qkv"][s, 0, RUN:, cols], lanes(RUN, width, offset))
            scores = nt(r["qkv"][s, 1, RUN:, cols], query) * (1.0 / math.sqrt(HEAD_DIM)) + r["bias_next"][...]
            r["soft_next"][8 * g + j] = jnp.exp(scores - r["stats_next"][s, 8 * g + j, :, :RUN])

    each_group(group)


def key_grads(s, r):
    def group(g, base):
        for j, start, width, offset in windows():
            cols = pl.ds(base + start, width)
            h = 8 * g + j
            keep = lanes(RUN, width, offset)
            flow = masked(r["flow"][s, 1, :, cols], keep)
            grad_soft = nt(r["qkv"][s, 2, RUN:, cols], flow)
            soft = r["soft_next"][h]
            grad = (soft * (grad_soft - r["stats_next"][2 + s, h, :, :RUN]) * (1.0 / math.sqrt(HEAD_DIM))).astype(
                jnp.bfloat16
            )
            softb = soft.astype(jnp.bfloat16)
            values = nn(r["softb"][h, :, :RUN], r["flow"][s, 0, :, cols]) + nn(softb, r["flow"][s, 1, :, cols])
            keys = nn(r["ds"][h, RUN:], r["qkv"][s, 0, :RUN, cols]) + nn(grad, r["qkv"][s, 0, RUN:, cols])
            kept_lanes(r["acc"].at[0], cols, keys, keep)
            kept_lanes(r["acc"].at[1], cols, values, keep)

    each_group(group)
    r["gqkv"][1] = r["acc"][0].astype(jnp.bfloat16)
    r["gqkv"][2] = r["acc"][1].astype(jnp.bfloat16)


def back_project(s, r, kinds, add):
    def chunk(n, _):
        rows = pl.ds(pl.multiple_of(256 * n, 256), 256)
        total = nt(r["gqkv"][kinds[0]], r["w"][s, kinds[0], rows, :])
        for t in kinds[1:]:
            total = total + nt(r["gqkv"][t], r["w"][s, t, rows, :])
        if add:
            total = total + r["gn"][:, rows]
        r["gn"][:, rows] = total

    lax.fori_loop(0, 5, chunk, None)


def input_grad(s, r):
    x = r["x"][s, 1].astype(jnp.float32)
    inverse = r["inverse"][s][:, :1]
    grad = r["gn"][...]
    r["terms"][s : s + 1] = jnp.sum(grad * x * inverse, axis=0, keepdims=True)
    scaled = grad * r["scale"][s]
    moved = inverse * (scaled - x * inverse * inverse * jnp.mean(scaled * x, axis=-1, keepdims=True))
    return (r["flow"][s, 0].astype(jnp.float32) + moved).astype(jnp.bfloat16)


NAMES = (
    "w", "x", "flow", "normed", "inverse", "qkv", "soft", "softb", "soft_next", "ds", "gqkv", "acc", "gn",
    "terms", "stats", "stats_next", "scale", "result",
)
SHAPES = [
    pltpu.VMEM((2, 3, WIDTH, WIDTH), jnp.bfloat16),
    pltpu.VMEM((2, 3, RUN, WIDTH), jnp.bfloat16),
    pltpu.VMEM((2, 2, RUN, WIDTH), jnp.bfloat16),
    pltpu.VMEM((3 * RUN, WIDTH), jnp.bfloat16),
    pltpu.VMEM((2, RUN, TILE), jnp.float32),
    pltpu.VMEM((2, 3, 2 * RUN, WIDTH), jnp.bfloat16),
    pltpu.VMEM((2, HEADS, 2 * RUN, RUN), jnp.float32),
    pltpu.VMEM((HEADS, RUN, TILE), jnp.bfloat16),
    pltpu.VMEM((HEADS, RUN, RUN), jnp.float32),
    pltpu.VMEM((HEADS, 2 * RUN, RUN), jnp.bfloat16),
    pltpu.VMEM((3, RUN, WIDTH), jnp.bfloat16),
    pltpu.VMEM((2, RUN, WIDTH), jnp.float32),
    pltpu.VMEM((RUN, WIDTH), jnp.float32),
    pltpu.VMEM((8, WIDTH), jnp.float32),
    pltpu.VMEM((4, HEADS, 1, TILE), jnp.float32),
    pltpu.VMEM((4, HEADS, 1, TILE), jnp.float32),
    pltpu.VMEM((2, 1, WIDTH), jnp.float32),
    pltpu.VMEM((2, RUN, WIDTH), jnp.bfloat16),
]
REDUCE_SCRATCH = [
    pltpu.VMEM((LAYERS, 8, TILE), jnp.float32),
    pltpu.VMEM((LAYERS, 8, TILE), jnp.float32),
    pltpu.VMEM((2, 8, TILE), jnp.float32),
    pltpu.VMEM((2 * PLANE, 8, TILE), jnp.float32),
    pltpu.SemaphoreType.DMA((LAYERS,)),
    pltpu.SemaphoreType.DMA((LAYERS,)),
    pltpu.SemaphoreType.DMA((2 * PLANE,)),
    pltpu.SemaphoreType.DMA((2 * PLANE,)),
]


def whole_kernel(raw, tokens, upstream, bias, bias_next, gains, out, gain_out, *scratch):
    r = dict(zip(NAMES, scratch[: len(NAMES)]))
    r["bias"], r["bias_next"] = bias, bias_next
    hsend, hrecv, local = scratch[len(NAMES) : len(NAMES) + 3]
    rest = scratch[len(NAMES) + 3 :]
    core, dp, z, slot, _, _ = place()
    load = pltpu.make_async_copy(tokens.at[core], r["x"].at[0, 1], local.at[0])
    load.start()
    load_up = pltpu.make_async_copy(upstream, r["flow"].at[1, 0], local.at[1])
    load_up.start()
    load_gain = pltpu.make_async_copy(gains, r["scale"].at[core], local.at[2])
    load_gain.start()
    greet(core, dp, z, slot)
    after, before = (dp + 1) % DEVICES, (dp + DEVICES - 1) % DEVICES

    def hand(k, source, target, c, d):
        return pltpu.make_async_remote_copy(
            src_ref=source,
            dst_ref=target,
            send_sem=hsend.at[k],
            recv_sem=hrecv.at[k],
            device_id=(c, d),
            device_id_type=MESH,
        )

    x, flow, stats, stats_next = r["x"], r["flow"], r["stats"], r["stats_next"]
    hands = []
    for s in range(2):
        hands.append(hand(4 * s, x.at[s, 1], x.at[s, 0], core, after))
        hands.append(hand(4 * s + 1, x.at[s, 1], x.at[s, 2], core, before))
        hands.append(hand(4 * s + 2, flow.at[s, 0], flow.at[s, 1], core, before))
        hands.append(hand(4 * s + 3, stats.at[s], stats_next.at[s], core, before))
    for s in range(2):
        hands.append(hand(8 + s, stats.at[2 + s], stats_next.at[2 + s], core, before))
    hands.append(hand(10, gains, r["scale"].at[core], 1 - core, dp))
    hands.append(hand(11, r["result"].at[1 - core], out.at[0, core], 1 - core, dp))
    hands[10].start()
    load.wait()
    hands[0].start()
    hands[1].start()
    load_up.wait()
    hands[6].start()
    load_gain.wait()
    drain = gather_body(raw, r["w"], *rest[: len(GATHER_SCRATCH)])
    hands[10].wait_recv()
    hands[0].wait_recv()
    hands[1].wait_recv()
    project(0, r)
    x[1, 1] = attend(0, r)
    hands[4].start()
    hands[5].start()
    hands[3].start()
    hands[4].wait_recv()
    hands[5].wait_recv()
    project(1, r)
    r["result"][1] = attend(1, r)
    hands[7].start()
    hands[6].wait_recv()
    for s in (1, 0):
        score_grads(s, r)
        hands[8 + s].start()
        query_grads(s, r)
        hands[4 * s + 3].wait_recv()
        next_soft(s, r)
        back_project(s, r, (0,), False)
        hands[8 + s].wait_recv()
        if s == 0:
            hands[2].wait_recv()
        key_grads(s, r)
        back_project(s, r, (1, 2), True)
        if s == 1:
            flow[0, 0] = input_grad(1, r)
            hands[2].start()
        else:
            r["result"][0] = input_grad(0, r)
    hands[11].start()
    keep = pltpu.make_async_copy(r["result"].at[core], out.at[0, core], local.at[3])
    keep.start()
    reduce_body(r["terms"], gain_out, *rest[len(GATHER_SCRATCH) :])
    keep.wait()
    hands[11].wait_recv()
    for h in hands:
        h.wait_send()
    drain()


def shards(tokens, segment_ids, loss_mask, qkv_weight, gains, cotangent):
    core = lax.axis_index("phase")
    dp = lax.axis_index("dp")
    raw = jnp.transpose(qkv_weight.reshape(5, 3, WIDTH), (1, 0, 2)).reshape(15, WIDTH)
    raw = jnp.pad(raw, ((0, 1), (0, 0)))
    runs = [jnp.clip(dp + k, 0, DEVICES - 1) * RUN for k in (-1, 0, 1)]
    seg_prev, seg_own, seg_next = (
        lax.dynamic_slice(segment_ids, (core, start), (1, RUN))[0] for start in runs
    )
    position = jnp.arange(RUN)
    own_ok = (seg_own[None, :] == seg_own[:, None]) & (position[:, None] <= position[None, :])
    prev_ok = (seg_own[None, :] == seg_prev[:, None]) & (dp > 0)
    next_ok = (seg_next[None, :] == seg_own[:, None]) & (dp < DEVICES - 1)
    bias = jnp.where(jnp.concatenate([prev_ok, own_ok], axis=0), 0.0, NEVER).astype(jnp.float32)
    bias_next = jnp.where(next_ok, 0.0, NEVER).astype(jnp.float32)
    chosen = lax.dynamic_index_in_dim(cotangent, core, 0, keepdims=False)
    mask = lax.dynamic_index_in_dim(loss_mask, core, 0, keepdims=False)
    upstream = jnp.where(mask[:, None] == 1, chosen, jnp.zeros((), jnp.bfloat16))
    vmem = pl.BlockSpec(memory_space=pltpu.VMEM)
    hbm = pl.BlockSpec(memory_space=pl.ANY)
    boundary, row = pl.pallas_call(
        whole_kernel,
        out_shape=(
            jax.ShapeDtypeStruct((1, 2, RUN, WIDTH), jnp.bfloat16),
            jax.ShapeDtypeStruct((1, TILE), jnp.float32),
        ),
        in_specs=[vmem, hbm, hbm, vmem, vmem, vmem],
        out_specs=(hbm, vmem),
        scratch_shapes=SHAPES
        + [pltpu.SemaphoreType.DMA((12,)), pltpu.SemaphoreType.DMA((12,)), pltpu.SemaphoreType.DMA((4,))]
        + GATHER_SCRATCH
        + REDUCE_SCRATCH,
        compiler_params=pltpu.CompilerParams(
            collective_id=0, has_side_effects=True, vmem_limit_bytes=56 * 2**20
        ),
        name="sections",
    )(raw, tokens, upstream, bias, bias_next, gains)
    slot = dp % PLANE
    return boundary, lax.dynamic_slice(row, (0, 5 * slot), (1, 5))


def solution(mesh):
    in_specs = (
        P(None, "dp", None),
        P(),
        P(None, "dp"),
        P("phase", "dp", None),
        P("phase", None),
        P(None, "dp", None),
    )
    out_specs = (P("phase", None, "dp", None), P("phase", "dp"))
    return jax.shard_map(shards, mesh=mesh, in_specs=in_specs, out_specs=out_specs, check_vma=False)
```

```python
import functools
import math

import jax
import jax.numpy as jnp
from jax import lax
from jax.experimental import pallas as pl
from jax.experimental.pallas import tpu as pltpu
from jax.sharding import PartitionSpec as P

WIDTH = 1280
HEADS = 16
HEAD_DIM = 80
RUN = 96
PLANE = 16
LAYERS = 16
SIDE = 4
PANEL = 80
TILE = 128
HALF = 640
RING_LAG = 4
CHIP_LAG = 8
DEVICES = 256
NEVER = -1e30
MESH = pl.DeviceIdType.MESH


def place():
    core = lax.axis_index("phase")
    dp = lax.axis_index("dp")
    z = dp // PLANE
    slot = dp % PLANE
    return core, dp, z, slot, slot // SIDE, slot % SIDE


def greet(core, dp, z, slot):
    barrier = pltpu.get_barrier_semaphore()
    mine = 2 * slot + core

    def plane(j, _):
        @pl.when(j != mine)
        def _():
            pl.semaphore_signal(barrier, inc=1, device_id=(j % 2, PLANE * z + j // 2), device_id_type=MESH)

    lax.fori_loop(0, 2 * PLANE, plane, None)

    def along(step, _):
        pl.semaphore_signal(
            barrier, inc=1, device_id=(core, PLANE * ((z + step) % LAYERS) + slot), device_id_type=MESH
        )

    lax.fori_loop(1, LAYERS, along, None)
    for step in (1, DEVICES - 1):
        pl.semaphore_signal(barrier, inc=1, device_id=(core, (dp + step) % DEVICES), device_id_type=MESH)
    pl.semaphore_wait(barrier, 2 * PLANE - 1 + LAYERS - 1 + 2)


def gather_body(prepare, raw, w, sendbuf, stage, psend, pown, precv, zsend, zrecv, rsend, rrecv, ssend, srecv):
    core, dp, z, slot, x, y = place()
    for c in range(2):
        for n in range(SIDE):
            sendbuf[c, n, :, :TILE] = raw[:, (5 * c + n) * TILE : (5 * c + n + 1) * TILE]
            sendbuf[c, n, :, TILE:] = raw[:, (5 * c + 4) * TILE : (5 * c + 5) * TILE]
    mine = 2 * slot + core

    def piece(j):
        c = j % 2
        i = j // 2
        n = jnp.where(c == 0, i % SIDE, i // SIDE)
        return pltpu.make_async_remote_copy(
            src_ref=sendbuf.at[c, n],
            dst_ref=stage.at[core, slot],
            send_sem=psend.at[j],
            recv_sem=precv.at[core],
            device_id=(c, PLANE * z + i),
            device_id_type=MESH,
        )

    ring_place = jnp.where(core == 0, y, x)
    own_piece = pltpu.make_async_copy(sendbuf.at[core, ring_place], stage.at[core, slot], precv.at[core])
    own_piece.start()

    def send_piece(j, _):
        @pl.when(j != mine)
        def _():
            piece(j).start()

    lax.fori_loop(0, 2 * PLANE, send_piece, None)
    prepare()
    base = 5 * core
    my_tile = base + ring_place
    row = lax.broadcasted_iota(jnp.int32, (3 * PANEL, 16 * PLANE), 0)
    column = lax.broadcasted_iota(jnp.int32, (3 * PANEL, 16 * PLANE), 1)
    within = row % PANEL
    wanted = (within // 5) * 16 + (row // PANEL) * 5 + within % 5
    select = (column == wanted).astype(jnp.float32).astype(jnp.bfloat16)
    rows = pl.ds(pl.multiple_of(PANEL * z, 16), PANEL)
    for s in range(2):
        pltpu.make_async_copy(stage.at[s], stage.at[s], precv.at[s]).wait()
        panel = jnp.dot(
            select, stage[s].reshape(16 * PLANE, 2 * TILE), preferred_element_type=jnp.float32
        ).astype(jnp.bfloat16)
        for t in range(3):
            w[s, t, rows, pl.ds(pl.multiple_of(TILE * my_tile, TILE), TILE)] = panel[
                t * PANEL : (t + 1) * PANEL, :TILE
            ]
            w[s, t, rows, pl.ds(pl.multiple_of(TILE * (base + 4), TILE), TILE)] = panel[
                t * PANEL : (t + 1) * PANEL, TILE:
            ]

    def drain_piece(j, _):
        @pl.when(j != mine)
        def _():
            piece(j).wait_send()

    lax.fori_loop(0, 2 * PLANE, drain_piece, None)

    def region(s, panel, tile, width=TILE):
        return w.at[
            s,
            :,
            pl.ds(pl.multiple_of(PANEL * panel, 16), PANEL),
            pl.ds(pl.multiple_of(TILE * tile, TILE), width),
        ]

    def tile_of(kind):
        return my_tile if kind == 0 else base + 4

    def panel_of(q):
        k = (q + 1) // 2
        sign = jnp.where(q % 2 == 1, -1, 1)
        return (z + sign * k + LAYERS) % LAYERS

    def z_copy(s, kind, panel, upward):
        to = (z + jnp.where(upward == 1, 1, LAYERS - 1)) % LAYERS
        piece_ref = region(s, panel, tile_of(kind))
        return pltpu.make_async_remote_copy(
            src_ref=piece_ref,
            dst_ref=piece_ref,
            send_sem=zsend.at[s, kind, upward, panel],
            recv_sem=zrecv.at[s, kind, panel],
            device_id=(core, PLANE * to + slot),
            device_id_type=MESH,
        )

    def ring_device(step):
        moved = (ring_place + step) % SIDE
        return PLANE * z + jnp.where(core == 0, SIDE * x + moved, SIDE * moved + y)

    def ring_tile(step):
        return base + (ring_place + step) % SIDE

    def ring_copy(s, panel, tile, step, way):
        piece_ref = region(s, panel, tile)
        return pltpu.make_async_remote_copy(
            src_ref=piece_ref,
            dst_ref=piece_ref,
            send_sem=rsend.at[s, panel, way],
            recv_sem=rrecv.at[s, panel, way],
            device_id=(core, ring_device(step)),
            device_id_type=MESH,
        )

    def passed_on(s, panel):
        even = panel % 2 == 0
        tile = jnp.where(even, ring_tile(SIDE - 1), ring_tile(1))
        return ring_copy(s, panel, tile, jnp.where(even, 1, SIDE - 1), 2)

    def sibling_copy(s, panel):
        piece_ref = region(s, panel, base, HALF)
        return pltpu.make_async_remote_copy(
            src_ref=piece_ref,
            dst_ref=piece_ref,
            send_sem=ssend.at[s, panel],
            recv_sem=srecv.at[s, panel],
            device_id=(1 - core, dp),
            device_id_type=MESH,
        )

    def step(i, _):
        @pl.when(i < 32)
        def _():
            s, q = i % 2, i // 2
            panel = panel_of(q)
            upward = q % 2

            @pl.when(q == 0)
            def _():
                for kind in range(2):
                    for way in range(2):
                        z_copy(s, kind, panel, way).start()

            @pl.when(q > 0)
            def _():
                z_copy(s, 0, panel, upward).wait_recv()

                @pl.when(q < 14)
                def _():
                    z_copy(s, 0, panel, upward).start()

                z_copy(s, 1, panel, upward).wait_recv()

                @pl.when((q < 13) | (q == 14))
                def _():
                    z_copy(s, 1, panel, upward).start()

            ring_copy(s, panel, my_tile, 1, 0).start()
            ring_copy(s, panel, my_tile, SIDE - 1, 1).start()

        @pl.when((i >= RING_LAG) & (i < 32 + RING_LAG))
        def _():
            s, q = (i - RING_LAG) % 2, (i - RING_LAG) // 2
            panel = panel_of(q)
            ring_copy(s, panel, ring_tile(SIDE - 1), 1, 0).wait_recv()
            ring_copy(s, panel, ring_tile(1), 1, 1).wait_recv()
            passed_on(s, panel).start()

        @pl.when(i >= CHIP_LAG)
        def _():
            s, q = (i - CHIP_LAG) % 2, (i - CHIP_LAG) // 2
            panel = panel_of(q)
            ring_copy(s, panel, ring_tile(2), 1, 2).wait_recv()
            sibling_copy(s, panel).start()

    lax.fori_loop(0, 32 + CHIP_LAG, step, None)

    def arrive(i, _):
        sibling_copy(i // 16, i % 16).wait_recv()

    lax.fori_loop(0, 32, arrive, None)

    def finish(i, _):
        s, q = i // 16, i % 16
        panel = panel_of(q)
        sibling_copy(s, panel).wait_send()

        for way in range(3):
            ring_copy(s, panel, my_tile, 1, way).wait_send()

        @pl.when(q == 0)
        def _():
            for kind in range(2):
                for way in range(2):
                    z_copy(s, kind, panel, way).wait_send()

        @pl.when((q > 0) & (q < 14))
        def _():
            z_copy(s, 0, panel, q % 2).wait_send()

        @pl.when(((q > 0) & (q < 13)) | (q == 14))
        def _():
            z_copy(s, 1, panel, q % 2).wait_send()

    return lambda: lax.fori_loop(0, 32, finish, None)


GATHER_SCRATCH = [
    pltpu.VMEM((2, SIDE, 16, 2 * TILE), jnp.bfloat16),
    pltpu.VMEM((2, PLANE, 16, 2 * TILE), jnp.bfloat16),
    pltpu.SemaphoreType.DMA((2 * PLANE,)),
    pltpu.SemaphoreType.DMA,
    pltpu.SemaphoreType.DMA((2,)),
    pltpu.SemaphoreType.DMA((2, 2, 2, LAYERS)),
    pltpu.SemaphoreType.DMA((2, 2, LAYERS)),
    pltpu.SemaphoreType.DMA((2, LAYERS, 3)),
    pltpu.SemaphoreType.DMA((2, LAYERS, 3)),
    pltpu.SemaphoreType.DMA((2, LAYERS)),
    pltpu.SemaphoreType.DMA((2, LAYERS)),
]


def reduce_body(terms, part, line, both, plane, lsend, lrecv, psend, precv):
    core, dp, z, slot, x, y = place()
    mine = 2 * slot + core

    def along(step):
        to = (z + step) % LAYERS
        return pltpu.make_async_remote_copy(
            src_ref=part.at[to],
            dst_ref=line.at[step],
            send_sem=lsend,
            recv_sem=lrecv,
            device_id=(core, PLANE * to + slot),
            device_id_type=MESH,
        )

    def across(j):
        return pltpu.make_async_remote_copy(
            src_ref=both.at[j % 2],
            dst_ref=plane.at[mine],
            send_sem=psend,
            recv_sem=precv,
            device_id=(j % 2, PLANE * z + j // 2),
            device_id_type=MESH,
        )

    def begin():
        for k in range(LAYERS):
            part[k, 0:2, :PANEL] = terms[0:2, PANEL * k : PANEL * (k + 1)]

        def start_along(step, _):
            along(step).start()

        lax.fori_loop(1, LAYERS, start_along, None)

    def end():
        batch = line.at[pl.ds(1, LAYERS - 1)]
        pltpu.make_async_copy(batch, batch, lrecv).wait()
        line[0, 0:2] = part[z, 0:2]
        total = jnp.sum(line[:, 0:2, :], axis=0)
        both[0, 0:1] = total[0:1]
        both[1, 0:1] = total[1:2]

        def start_across(j, _):
            @pl.when(j != mine)
            def _():
                across(j).start()

        lax.fori_loop(0, 2 * PLANE, start_across, None)
        pltpu.make_async_copy(batch, batch, lsend).wait()
        own = pltpu.make_async_copy(both.at[core], plane.at[mine], precv)
        own.start()
        pltpu.make_async_copy(plane, plane, precv).wait()
        row = jnp.sum(plane[:, 0:1, :], axis=0)
        others = plane.at[pl.ds(0, 2 * PLANE - 1)]
        pltpu.make_async_copy(others, others, psend).wait()
        return row, slot

    return begin, end


def eye(n):
    return lax.broadcasted_iota(jnp.int32, (n, n), 0) == lax.broadcasted_iota(jnp.int32, (n, n), 1)


def down(row):
    return jnp.sum(jnp.where(eye(row.shape[1]), row, 0.0), axis=1, keepdims=True)


def across_lanes(column):
    return jnp.sum(jnp.where(eye(column.shape[0]), column, 0.0), axis=0, keepdims=True)


def labels_of(segments, core, run):
    first = RUN * run
    start = jnp.minimum(first // TILE * TILE, RUN * DEVICES - 2 * TILE)
    window = segments[pl.ds(core, 1), pl.ds(pl.multiple_of(start, TILE), 2 * TILE)].astype(jnp.float32)
    row = lax.broadcasted_iota(jnp.int32, (RUN, 2 * TILE), 0)
    lane = lax.broadcasted_iota(jnp.int32, (RUN, 2 * TILE), 1)
    return jnp.sum(jnp.where(lane == row + (first - start), window, 0.0), axis=1, keepdims=True)


def fill_biases(segments, bias, bias_next):
    core, dp, _, _, _, _ = place()
    own = labels_of(segments, core, dp)
    prev = labels_of(segments, core, jnp.maximum(dp - 1, 0))
    after = labels_of(segments, core, jnp.minimum(dp + 1, DEVICES - 1))
    own_row, after_row = across_lanes(own), across_lanes(after)
    key = lax.broadcasted_iota(jnp.int32, (RUN, RUN), 0)
    query = lax.broadcasted_iota(jnp.int32, (RUN, RUN), 1)
    never = jnp.float32(NEVER)
    bias[:RUN] = jnp.where((prev == own_row) & (dp > 0), 0.0, never)
    bias[RUN:] = jnp.where((own == own_row) & (key <= query), 0.0, never)
    bias_next[...] = jnp.where((own == after_row) & (dp < DEVICES - 1), 0.0, never)


def windows():
    for j in range(8):
        first = HEAD_DIM * j
        start = first // TILE * TILE
        stop = -(-(first + HEAD_DIM) // TILE) * TILE
        yield j, start, stop - start, first - start


def lanes(rows, width, offset):
    lane = lax.broadcasted_iota(jnp.int32, (rows, width), 1)
    return (lane >= offset) & (lane < offset + HEAD_DIM)


def nt(a, b):
    return lax.dot_general(a, b, (((1,), (1,)), ((), ())), preferred_element_type=jnp.float32)


def tn(a, b):
    return lax.dot_general(a, b, (((0,), (0,)), ((), ())), preferred_element_type=jnp.float32)


def nn(a, b):
    return jnp.dot(a, b, preferred_element_type=jnp.float32)


def each_group(body):
    lax.fori_loop(0, 2, lambda g, _: body(g, pl.multiple_of(HALF * g, TILE)), None)


def kept_lanes(ref, cols, value, keep):
    ref[:, cols] = jnp.where(keep, value, ref[:, cols])


def masked(value, keep):
    return jnp.where(keep, value, jnp.zeros((), value.dtype))


def project(s, r):
    x = r["x"][s].reshape(3 * RUN, WIDTH).astype(jnp.float32)
    inverse = lax.rsqrt(jnp.mean(x * x, axis=-1, keepdims=True) + 1e-05)
    r["normed"][...] = (x * inverse * r["scale"][s]).astype(jnp.bfloat16)
    r["inverse"][s] = jnp.broadcast_to(inverse[RUN : 2 * RUN], (RUN, TILE))
    for t, first in ((0, RUN), (1, 0), (2, 0)):

        def chunk(n, _):
            cols = pl.ds(pl.multiple_of(HALF * n, TILE), HALF)
            r["qkv"][s, t, :, cols] = nn(r["normed"][first : first + 2 * RUN], r["w"][s, t, :, cols]).astype(
                jnp.bfloat16
            )

        lax.fori_loop(0, 2, chunk, None)


def attend(s, r, done):
    att = r["acc"].at[0]

    def group(g, base):
        for j, start, width, offset in windows():
            cols = pl.ds(base + start, width)
            keep = lanes(RUN, width, offset)
            query = masked(r["qkv"][s, 0, :RUN, cols], keep)
            scores = nt(r["qkv"][s, 1, :, cols], query) * (1.0 / math.sqrt(HEAD_DIM)) + r["bias"][...]
            highest = jnp.max(scores, axis=0, keepdims=True)
            exponent = jnp.exp(scores - highest)
            total = jnp.sum(exponent, axis=0, keepdims=True)
            soft = exponent / total
            r["soft"][s, 8 * g + j] = soft
            r["stats"][s, 8 * g + j, :, :RUN] = highest + jnp.log(total)
            kept_lanes(att, cols, tn(soft.astype(jnp.bfloat16), r["qkv"][s, 2, :, cols]), keep)

    for g in range(2):
        group(g, HALF * g)
        done(g)


def score_grads(s, r):
    def group(g, base):
        for j, start, width, offset in windows():
            cols = pl.ds(base + start, width)
            h = 8 * g + j
            flow = masked(r["flow"][s, 0, :, cols], lanes(RUN, width, offset))
            grad_soft = nt(r["qkv"][s, 2, :, cols], flow)
            soft = r["soft"][s, h]
            inner = jnp.sum(soft * grad_soft, axis=0, keepdims=True)
            r["stats"][2 + s, h, :, :RUN] = inner
            grad = (soft * (grad_soft - inner) * (1.0 / math.sqrt(HEAD_DIM))).astype(jnp.bfloat16)
            r["ds"][h] = grad
            r["softb"][h, :, :RUN] = soft[RUN:].astype(jnp.bfloat16)

    each_group(group)


def query_grads(s, r):
    def group(g, base):
        for j, start, width, offset in windows():
            cols = pl.ds(base + start, width)
            keep = lanes(RUN, width, offset)
            kept_lanes(r["acc"].at[0], cols, tn(r["ds"][8 * g + j], r["qkv"][s, 1, :, cols]), keep)

    each_group(group)
    r["gqkv"][0] = r["acc"][0].astype(jnp.bfloat16)


def next_soft(s, r):
    def group(g, base):
        for j, start, width, offset in windows():
            cols = pl.ds(base + start, width)
            query = masked(r["qkv"][s, 0, RUN:, cols], lanes(RUN, width, offset))
            scores = nt(r["qkv"][s, 1, RUN:, cols], query) * (1.0 / math.sqrt(HEAD_DIM)) + r["bias_next"][...]
            r["soft_next"][8 * g + j] = jnp.exp(scores - r["stats_next"][s, 8 * g + j, :, :RUN])

    each_group(group)


def key_grads(s, r):
    def group(g, base):
        for j, start, width, offset in windows():
            cols = pl.ds(base + start, width)
            h = 8 * g + j
            keep = lanes(RUN, width, offset)
            flow = masked(r["flow"][s, 1, :, cols], keep)
            grad_soft = nt(r["qkv"][s, 2, RUN:, cols], flow)
            soft = r["soft_next"][h]
            grad = (soft * (grad_soft - r["stats_next"][2 + s, h, :, :RUN]) * (1.0 / math.sqrt(HEAD_DIM))).astype(
                jnp.bfloat16
            )
            softb = soft.astype(jnp.bfloat16)
            values = nn(r["softb"][h, :, :RUN], r["flow"][s, 0, :, cols]) + nn(softb, r["flow"][s, 1, :, cols])
            keys = nn(r["ds"][h, RUN:], r["qkv"][s, 0, :RUN, cols]) + nn(grad, r["qkv"][s, 0, RUN:, cols])
            kept_lanes(r["acc"].at[0], cols, keys, keep)
            kept_lanes(r["acc"].at[1], cols, values, keep)

    each_group(group)
    r["gqkv"][1] = r["acc"][0].astype(jnp.bfloat16)
    r["gqkv"][2] = r["acc"][1].astype(jnp.bfloat16)


def back_project(s, r, kinds, add):
    def chunk(n, _):
        rows = pl.ds(pl.multiple_of(HALF * n, TILE), HALF)
        total = nt(r["gqkv"][kinds[0]], r["w"][s, kinds[0], rows, :])
        for t in kinds[1:]:
            total = total + nt(r["gqkv"][t], r["w"][s, t, rows, :])
        if add:
            total = total + r["gn"][:, rows]
        r["gn"][:, rows] = total

    lax.fori_loop(0, 2, chunk, None)


def gain_terms(s, r):
    x = r["x"][s, 1].astype(jnp.float32)
    r["terms"][s : s + 1] = jnp.sum(r["gn"][...] * x * r["inverse"][s][:, :1], axis=0, keepdims=True)


def input_grad(s, r):
    x = r["x"][s, 1].astype(jnp.float32)
    inverse = r["inverse"][s][:, :1]
    grad = r["gn"][...]
    scaled = grad * r["scale"][s]
    moved = inverse * (scaled - x * inverse * inverse * jnp.mean(scaled * x, axis=-1, keepdims=True))
    return (r["flow"][s, 0].astype(jnp.float32) + moved).astype(jnp.bfloat16)


NAMES = (
    "w", "x", "flow", "normed", "inverse", "qkv", "soft", "softb", "soft_next", "ds", "gqkv", "acc", "gn",
    "terms", "stats", "stats_next", "scale", "result", "bias", "bias_next", "raw",
)
SHAPES = [
    pltpu.VMEM((2, 3, WIDTH, WIDTH), jnp.bfloat16),
    pltpu.VMEM((2, 3, RUN, WIDTH), jnp.bfloat16),
    pltpu.VMEM((2, 2, RUN, WIDTH), jnp.bfloat16),
    pltpu.VMEM((3 * RUN, WIDTH), jnp.bfloat16),
    pltpu.VMEM((2, RUN, TILE), jnp.float32),
    pltpu.VMEM((2, 3, 2 * RUN, WIDTH), jnp.bfloat16),
    pltpu.VMEM((2, HEADS, 2 * RUN, RUN), jnp.float32),
    pltpu.VMEM((HEADS, RUN, TILE), jnp.bfloat16),
    pltpu.VMEM((HEADS, RUN, RUN), jnp.float32),
    pltpu.VMEM((HEADS, 2 * RUN, RUN), jnp.bfloat16),
    pltpu.VMEM((3, RUN, WIDTH), jnp.bfloat16),
    pltpu.VMEM((2, RUN, WIDTH), jnp.float32),
    pltpu.VMEM((RUN, WIDTH), jnp.float32),
    pltpu.VMEM((8, WIDTH), jnp.float32),
    pltpu.VMEM((4, HEADS, 1, TILE), jnp.float32),
    pltpu.VMEM((4, HEADS, 1, TILE), jnp.float32),
    pltpu.VMEM((2, 1, WIDTH), jnp.float32),
    pltpu.VMEM((2, RUN, WIDTH), jnp.bfloat16),
    pltpu.VMEM((2 * RUN, RUN), jnp.float32),
    pltpu.VMEM((RUN, RUN), jnp.float32),
    pltpu.VMEM((16, WIDTH), jnp.bfloat16),
]
REDUCE_SCRATCH = [
    pltpu.VMEM((LAYERS, 8, TILE), jnp.float32),
    pltpu.VMEM((LAYERS, 8, TILE), jnp.float32),
    pltpu.VMEM((2, 8, TILE), jnp.float32),
    pltpu.VMEM((2 * PLANE, 8, TILE), jnp.float32),
    pltpu.SemaphoreType.DMA,
    pltpu.SemaphoreType.DMA,
    pltpu.SemaphoreType.DMA,
    pltpu.SemaphoreType.DMA,
]


def whole_kernel(shard, tokens, segments, mask, cotangent, gains, out, gain_out, *scratch):
    r = dict(zip(NAMES, scratch[: len(NAMES)]))
    hsend, hrecv, local = scratch[len(NAMES) : len(NAMES) + 3]
    rest = scratch[len(NAMES) + 3 :]
    core, dp, z, slot, _, _ = place()
    load = pltpu.make_async_copy(tokens.at[core], r["x"].at[0, 1], local.at[0])
    load.start()
    load_up = pltpu.make_async_copy(cotangent.at[core], r["flow"].at[1, 0], local.at[1])
    load_up.start()
    load_gain = pltpu.make_async_copy(gains, r["scale"].at[core], local.at[2])
    load_gain.start()
    wide = shard[0].astype(jnp.float32)
    parts = [wide[:, WIDTH * t : WIDTH * (t + 1)] for t in range(3)]
    r["raw"][...] = jnp.concatenate(parts + [jnp.zeros((1, WIDTH), jnp.float32)], axis=0).astype(jnp.bfloat16)
    greet(core, dp, z, slot)
    after, before = (dp + 1) % DEVICES, (dp + DEVICES - 1) % DEVICES

    def hand(k, source, target, c, d):
        return pltpu.make_async_remote_copy(
            src_ref=source,
            dst_ref=target,
            send_sem=hsend.at[k],
            recv_sem=hrecv.at[k],
            device_id=(c, d),
            device_id_type=MESH,
        )

    x, flow, stats, stats_next = r["x"], r["flow"], r["stats"], r["stats_next"]
    give_scale = hand(0, gains, r["scale"].at[core], 1 - core, dp)
    give_result = hand(1, r["result"].at[1 - core], out.at[0, core], 1 - core, dp)
    give_first = [hand(2, x.at[0, 1], x.at[0, 0], core, after), hand(3, x.at[0, 1], x.at[0, 2], core, before)]
    give_flow = [hand(4 + s, flow.at[s, 0], flow.at[s, 1], core, before) for s in range(2)]
    give_lse = [hand(6 + s, stats.at[s], stats_next.at[s], core, before) for s in range(2)]
    give_inner = [hand(8 + s, stats.at[2 + s], stats_next.at[2 + s], core, before) for s in range(2)]
    give_middle = []
    for g in range(2):
        cols = pl.ds(HALF * g, HALF)
        give_middle.append(hand(10 + 2 * g, x.at[1, 1, :, cols], x.at[1, 0, :, cols], core, after))
        give_middle.append(hand(11 + 2 * g, x.at[1, 1, :, cols], x.at[1, 2, :, cols], core, before))
    give_scale.start()
    load.wait()
    for h in give_first:
        h.start()

    def prepare():
        load_up.wait()
        chosen = down(mask[pl.ds(core, 1), :].astype(jnp.float32)) == 1.0
        flow[1, 0] = jnp.where(chosen, flow[1, 0].astype(jnp.float32), 0.0).astype(jnp.bfloat16)
        give_flow[1].start()
        load_gain.wait()
        fill_biases(segments, r["bias"], r["bias_next"])

    drain = gather_body(prepare, r["raw"], r["w"], *rest[: len(GATHER_SCRATCH)])
    begin, end = reduce_body(r["terms"], *rest[len(GATHER_SCRATCH) :])
    give_scale.wait_recv()
    for h in give_first:
        h.wait_recv()
    project(0, r)

    def middle(g):
        cols = slice(HALF * g, HALF * (g + 1))
        x[1, 1, :, cols] = (x[0, 1, :, cols].astype(jnp.float32) + r["acc"][0, :, cols]).astype(jnp.bfloat16)
        give_middle[2 * g].start()
        give_middle[2 * g + 1].start()

    attend(0, r, middle)
    give_lse[0].start()
    drain()
    for h in give_middle:
        h.wait_recv()
    project(1, r)

    def final(g):
        cols = slice(HALF * g, HALF * (g + 1))
        r["result"][1, :, cols] = (x[1, 1, :, cols].astype(jnp.float32) + r["acc"][0, :, cols]).astype(jnp.bfloat16)

    attend(1, r, final)
    give_lse[1].start()
    give_flow[1].wait_recv()
    for s in (1, 0):
        score_grads(s, r)
        give_inner[s].start()
        query_grads(s, r)
        give_lse[s].wait_recv()
        next_soft(s, r)
        back_project(s, r, (0,), False)
        give_inner[s].wait_recv()
        if s == 0:
            give_flow[0].wait_recv()
        key_grads(s, r)
        back_project(s, r, (1, 2), True)
        gain_terms(s, r)
        if s == 1:
            flow[0, 0] = input_grad(1, r)
            give_flow[0].start()
        else:
            begin()
            r["result"][0] = input_grad(0, r)
    give_result.start()
    keep = pltpu.make_async_copy(r["result"].at[core], out.at[0, core], local.at[3])
    keep.start()
    row, slot = end()
    spread = down(row)
    sub = lax.broadcasted_iota(jnp.int32, (TILE, TILE), 0)
    lane = lax.broadcasted_iota(jnp.int32, (TILE, TILE), 1)
    gain_out[...] = jnp.sum(jnp.where(sub == lane + 5 * slot, spread, 0.0), axis=0, keepdims=True)[:, :5]
    keep.wait()
    give_result.wait_recv()
    for h in [give_scale, give_result] + give_first + give_flow + give_lse + give_inner + give_middle:
        h.wait_send()


def shards(tokens, segment_ids, loss_mask, qkv_weight, gains, cotangent):
    vmem = pl.BlockSpec(memory_space=pltpu.VMEM)
    hbm = pl.BlockSpec(memory_space=pl.ANY)
    return pl.pallas_call(
        whole_kernel,
        out_shape=(
            jax.ShapeDtypeStruct((1, 2, RUN, WIDTH), jnp.bfloat16),
            jax.ShapeDtypeStruct((1, 5), jnp.float32),
        ),
        in_specs=[vmem, hbm, vmem, vmem, hbm, vmem],
        out_specs=(hbm, vmem),
        scratch_shapes=SHAPES
        + [pltpu.SemaphoreType.DMA((14,)), pltpu.SemaphoreType.DMA((14,)), pltpu.SemaphoreType.DMA((4,))]
        + GATHER_SCRATCH
        + REDUCE_SCRATCH,
        compiler_params=pltpu.CompilerParams(
            collective_id=0, has_side_effects=True, vmem_limit_bytes=56 * 2**20
        ),
        name="sections",
    )(qkv_weight, tokens, segment_ids, loss_mask, cotangent, gains)


def solution(mesh):
    in_specs = (
        P(None, "dp", None),
        P(),
        P(None, "dp"),
        P("phase", "dp", None),
        P("phase", None),
        P(None, "dp", None),
    )
    out_specs = (P("phase", None, "dp", None), P("phase", "dp"))
    return jax.shard_map(shards, mesh=mesh, in_specs=in_specs, out_specs=out_specs, check_vma=False)
```

```python
import functools
import math

import jax
import jax.numpy as jnp
from jax import lax
from jax.experimental import pallas as pl
from jax.experimental.pallas import tpu as pltpu
from jax.sharding import PartitionSpec as P

WIDTH = 1280
HEADS = 16
HEAD_DIM = 80
RUN = 96
PLANE = 16
LAYERS = 16
SIDE = 4
PANEL = 80
TILE = 128
HALF = 640
LEAD = 0
RING_LAG = 1
CHIP_LAG = 3
DEVICES = 256
NEVER = -1e30
PIECES = ((0, 384), (384, 256), (640, 384), (1024, 256))
MESH = pl.DeviceIdType.MESH


def place():
    core = lax.axis_index("phase")
    dp = lax.axis_index("dp")
    z = lax.div(dp, PLANE)
    slot = lax.rem(dp, PLANE)
    return core, dp, z, slot, lax.div(slot, SIDE), lax.rem(slot, SIDE)


def greet(core, dp, z, slot):
    barrier = pltpu.get_barrier_semaphore()
    mine = 2 * slot + core

    def plane(j, _):
        @pl.when(j != mine)
        def _():
            pl.semaphore_signal(barrier, inc=1, device_id=(j % 2, PLANE * z + j // 2), device_id_type=MESH)

    lax.fori_loop(0, 2 * PLANE, plane, None)

    def along(step, _):
        pl.semaphore_signal(
            barrier, inc=1, device_id=(core, PLANE * ((z + step) % LAYERS) + slot), device_id_type=MESH
        )

    lax.fori_loop(1, LAYERS, along, None)
    for step in (1, DEVICES - 1):
        pl.semaphore_signal(barrier, inc=1, device_id=(core, (dp + step) % DEVICES), device_id_type=MESH)
    pl.semaphore_wait(barrier, 2 * PLANE - 1 + LAYERS - 1 + 2)


def gather_body(prepare, fill, raw, w, sendbuf, stage, psend, pown, precv, zsend, zrecv, rsend, rrecv, ssend, srecv):
    core, dp, z, slot, x, y = place()
    for c in range(2):
        for n in range(SIDE):
            sendbuf[c, n, :, :TILE] = raw[:, (5 * c + n) * TILE : (5 * c + n + 1) * TILE]
            sendbuf[c, n, :, TILE:] = raw[:, (5 * c + 4) * TILE : (5 * c + 5) * TILE]
    mine = 2 * slot + core

    def piece(j):
        c = j % 2
        i = j // 2
        n = jnp.where(c == 0, i % SIDE, i // SIDE)
        return pltpu.make_async_remote_copy(
            src_ref=sendbuf.at[c, n],
            dst_ref=stage.at[core, slot],
            send_sem=psend.at[j],
            recv_sem=precv.at[core],
            device_id=(c, PLANE * z + i),
            device_id_type=MESH,
        )

    ring_place = jnp.where(core == 0, y, x)
    own_piece = pltpu.make_async_copy(sendbuf.at[core, ring_place], stage.at[core, slot], precv.at[core])
    own_piece.start()

    def send_piece(j, _):
        @pl.when(j != mine)
        def _():
            piece(j).start()

    lax.fori_loop(0, 2 * PLANE, send_piece, None)
    base = 5 * core
    my_tile = base + ring_place
    row = lax.broadcasted_iota(jnp.int32, (3 * PANEL, 16 * PLANE), 0)
    column = lax.broadcasted_iota(jnp.int32, (3 * PANEL, 16 * PLANE), 1)
    within = row % PANEL
    wanted = (within // 5) * 16 + (row // PANEL) * 5 + within % 5
    select = (column == wanted).astype(jnp.float32).astype(jnp.bfloat16)
    rows = pl.ds(pl.multiple_of(PANEL * z, 16), PANEL)
    def retile(s):
        pltpu.make_async_copy(stage.at[s], stage.at[s], precv.at[s]).wait()
        panel = jnp.dot(
            select, stage[s].reshape(16 * PLANE, 2 * TILE), preferred_element_type=jnp.float32
        ).astype(jnp.bfloat16)
        for t in range(3):
            w[s, t, rows, pl.ds(pl.multiple_of(TILE * my_tile, TILE), TILE)] = panel[
                t * PANEL : (t + 1) * PANEL, :TILE
            ]
            w[s, t, rows, pl.ds(pl.multiple_of(TILE * (base + 4), TILE), TILE)] = panel[
                t * PANEL : (t + 1) * PANEL, TILE:
            ]

    def drain_piece(j, _):
        @pl.when(j != mine)
        def _():
            piece(j).wait_send()

    def region(s, panel, tile, width=TILE):
        return w.at[
            s,
            :,
            pl.ds(pl.multiple_of(PANEL * panel, 16), PANEL),
            pl.ds(pl.multiple_of(TILE * tile, TILE), width),
        ]

    def wrapped(value, size):
        return lax.rem(value, size)

    def panel_of(q):
        k = lax.div(q + 1, 2)
        return wrapped(z + LAYERS + (1 - 2 * lax.rem(q, 2)) * k, LAYERS)

    line_devices = [PLANE * wrapped(z + LAYERS + move, LAYERS) + slot for move in (-1, 1)]
    ring_steps = [wrapped(ring_place + step, SIDE) for step in range(SIDE)]
    ring_tiles = [base + moved for moved in ring_steps]
    ring_devices = [
        PLANE * z + jnp.where(core == 0, SIDE * x + moved, SIDE * moved + y) for moved in ring_steps
    ]
    tiles = (my_tile, base + 4)

    def z_copy(s, kind, panel, q, to):
        piece_ref = region(s, panel, tiles[kind])
        return pltpu.make_async_remote_copy(
            src_ref=piece_ref,
            dst_ref=piece_ref,
            send_sem=zsend.at[s, kind, q],
            recv_sem=zrecv.at[s, kind, q],
            device_id=(core, to),
            device_id_type=MESH,
        )

    def ring_copy(s, panel, q, tile, to, way):
        piece_ref = region(s, panel, tile)
        return pltpu.make_async_remote_copy(
            src_ref=piece_ref,
            dst_ref=piece_ref,
            send_sem=rsend.at[s, q, way],
            recv_sem=rrecv.at[s, q, way],
            device_id=(core, to),
            device_id_type=MESH,
        )

    def sibling_copy(s, panel, q):
        piece_ref = region(s, panel, base, HALF)
        return pltpu.make_async_remote_copy(
            src_ref=piece_ref,
            dst_ref=piece_ref,
            send_sem=ssend.at[s, q],
            recv_sem=srecv.at[s, q],
            device_id=(1 - core, dp),
            device_id_type=MESH,
        )

    def start_rings(s, panel, q):
        ring_copy(s, panel, q, my_tile, ring_devices[1], 0).start()
        ring_copy(s, panel, q, my_tile, ring_devices[3], 1).start()

    def begin(s):
        for kind in range(2):
            for way in range(2):
                z_copy(s, kind, z, 1 + way, line_devices[1 - way]).start()
        start_rings(s, z, 0)

    for s in range(2):
        retile(s)
        if LEAD == 0 or s == 0:
            begin(s)
    prepare()

    def step(i, _):
        for s in range(2):
            q = i - LEAD * s

            if LEAD > 0 and s == 1:

                @pl.when(q == 0)
                def _():
                    begin(1)

            @pl.when((q >= 1) & (q < 16))
            def _():
                panel = panel_of(q)
                to = jnp.where(lax.rem(q, 2) == 1, line_devices[1], line_devices[0])
                z_copy(s, 0, panel, q, to).wait_recv()

                @pl.when(q < 14)
                def _():
                    z_copy(s, 0, panel, q + 2, to).start()

                z_copy(s, 1, panel, q, to).wait_recv()

                @pl.when((q < 13) | (q == 14))
                def _():
                    z_copy(s, 1, panel, q + 2 - lax.div(q, 14), to).start()

                start_rings(s, panel, q)

        for s in range(2):
            passing = i - LEAD * s - RING_LAG

            @pl.when((passing >= 0) & (passing < 16))
            def _():
                panel = panel_of(passing)
                even = lax.rem(panel, 2) == 0
                tile = jnp.where(even, ring_tiles[3], ring_tiles[1])
                to = jnp.where(even, ring_devices[1], ring_devices[3])
                ring_copy(s, panel, passing, ring_tiles[3], to, 0).wait_recv()
                ring_copy(s, panel, passing, ring_tiles[1], to, 1).wait_recv()
                ring_copy(s, panel, passing, tile, to, 2).start()

        for s in range(2):
            complete = i - LEAD * s - CHIP_LAG

            @pl.when((complete >= 0) & (complete < 16))
            def _():
                panel = panel_of(complete)
                ring_copy(s, panel, complete, ring_tiles[2], dp, 2).wait_recv()
                sibling_copy(s, panel, complete).start()

    def arrived(s):
        def one(q, _):
            sibling_copy(s, panel_of(q), q).wait_recv()

        lax.fori_loop(0, 16, one, None)

    lax.fori_loop(1, 16 + LEAD, step, None)
    if CHIP_LAG <= LEAD:
        arrived(0)
        fill(0)
        for n in range(CHIP_LAG):
            lax.fori_loop(16 + LEAD + n, 17 + LEAD + n, step, None)
            fill(n + 1)
    else:
        lax.fori_loop(16 + LEAD, 16 + LEAD + CHIP_LAG, step, None)
        arrived(0)
        for n in range(3):
            fill(n)
    arrived(1)

    def finish(q, _):
        panel = panel_of(q)
        for s in range(2):
            sibling_copy(s, panel, q).wait_send()
            for way in range(3):
                ring_copy(s, panel, q, my_tile, dp, way).wait_send()
            for kind in range(2):

                @pl.when(q > 0)
                def _():
                    z_copy(s, kind, panel, q, dp).wait_send()

    def drain():
        lax.fori_loop(0, 2 * PLANE, drain_piece, None)
        lax.fori_loop(0, 16, finish, None)

    return drain


GATHER_SCRATCH = [
    pltpu.VMEM((2, SIDE, 16, 2 * TILE), jnp.bfloat16),
    pltpu.VMEM((2, PLANE, 16, 2 * TILE), jnp.bfloat16),
    pltpu.SemaphoreType.DMA((2 * PLANE,)),
    pltpu.SemaphoreType.DMA,
    pltpu.SemaphoreType.DMA((2,)),
    pltpu.SemaphoreType.DMA((2, 2, LAYERS)),
    pltpu.SemaphoreType.DMA((2, 2, LAYERS)),
    pltpu.SemaphoreType.DMA((2, LAYERS, 3)),
    pltpu.SemaphoreType.DMA((2, LAYERS, 3)),
    pltpu.SemaphoreType.DMA((2, LAYERS)),
    pltpu.SemaphoreType.DMA((2, LAYERS)),
]


def reduce_body(terms, part, line, both, plane, lsend, lrecv, psend, precv):
    core, dp, z, slot, x, y = place()
    mine = 2 * slot + core

    def along(step):
        to = (z + step) % LAYERS
        return pltpu.make_async_remote_copy(
            src_ref=part.at[to],
            dst_ref=line.at[step],
            send_sem=lsend,
            recv_sem=lrecv,
            device_id=(core, PLANE * to + slot),
            device_id_type=MESH,
        )

    def across(j):
        return pltpu.make_async_remote_copy(
            src_ref=both.at[j % 2],
            dst_ref=plane.at[mine],
            send_sem=psend,
            recv_sem=precv,
            device_id=(j % 2, PLANE * z + j // 2),
            device_id_type=MESH,
        )

    def begin():
        for k in range(LAYERS):
            part[k, 0:2, :PANEL] = terms[0:2, PANEL * k : PANEL * (k + 1)]

        def start_along(step, _):
            along(step).start()

        lax.fori_loop(1, LAYERS, start_along, None)

    def end():
        batch = line.at[pl.ds(1, LAYERS - 1)]
        pltpu.make_async_copy(batch, batch, lrecv).wait()
        line[0, 0:2] = part[z, 0:2]
        total = jnp.sum(line[:, 0:2, :], axis=0)
        both[0, 0:1] = total[0:1]
        both[1, 0:1] = total[1:2]

        def start_across(j, _):
            @pl.when(j != mine)
            def _():
                across(j).start()

        lax.fori_loop(0, 2 * PLANE, start_across, None)
        pltpu.make_async_copy(batch, batch, lsend).wait()
        own = pltpu.make_async_copy(both.at[core], plane.at[mine], precv)
        own.start()
        pltpu.make_async_copy(plane, plane, precv).wait()
        row = jnp.sum(plane[:, 0:1, :], axis=0)
        others = plane.at[pl.ds(0, 2 * PLANE - 1)]
        pltpu.make_async_copy(others, others, psend).wait()
        return row, slot

    return begin, end


def eye(n):
    return lax.broadcasted_iota(jnp.int32, (n, n), 0) == lax.broadcasted_iota(jnp.int32, (n, n), 1)


def down(row):
    return jnp.sum(jnp.where(eye(row.shape[1]), row, 0.0), axis=1, keepdims=True)


def across_lanes(column):
    return jnp.sum(jnp.where(eye(column.shape[0]), column, 0.0), axis=0, keepdims=True)


def labels_of(segments, core, run):
    first = RUN * run
    start = jnp.minimum(first // TILE * TILE, RUN * DEVICES - 2 * TILE)
    window = segments[pl.ds(core, 1), pl.ds(pl.multiple_of(start, TILE), 2 * TILE)].astype(jnp.float32)
    row = lax.broadcasted_iota(jnp.int32, (RUN, 2 * TILE), 0)
    lane = lax.broadcasted_iota(jnp.int32, (RUN, 2 * TILE), 1)
    return jnp.sum(jnp.where(lane == row + (first - start), window, 0.0), axis=1, keepdims=True)


def fill_biases(segments, bias, bias_next):
    core, dp, _, _, _, _ = place()
    own = labels_of(segments, core, dp)
    prev = labels_of(segments, core, jnp.maximum(dp - 1, 0))
    after = labels_of(segments, core, jnp.minimum(dp + 1, DEVICES - 1))
    own_row, after_row = across_lanes(own), across_lanes(after)
    key = lax.broadcasted_iota(jnp.int32, (RUN, RUN), 0)
    query = lax.broadcasted_iota(jnp.int32, (RUN, RUN), 1)
    never = jnp.float32(NEVER)
    bias[:RUN] = jnp.where((prev == own_row) & (dp > 0), 0.0, never)
    bias[RUN:] = jnp.where((own == own_row) & (key <= query), 0.0, never)
    bias_next[...] = jnp.where((own == after_row) & (dp < DEVICES - 1), 0.0, never)


def windows():
    for j in range(8):
        first = HEAD_DIM * j
        start = first // TILE * TILE
        stop = -(-(first + HEAD_DIM) // TILE) * TILE
        yield j, start, stop - start, first - start


def lanes(rows, width, offset):
    lane = lax.broadcasted_iota(jnp.int32, (rows, width), 1)
    return (lane >= offset) & (lane < offset + HEAD_DIM)


def nt(a, b):
    return lax.dot_general(a, b, (((1,), (1,)), ((), ())), preferred_element_type=jnp.float32)


def tn(a, b):
    return lax.dot_general(a, b, (((0,), (0,)), ((), ())), preferred_element_type=jnp.float32)


def nn(a, b):
    return jnp.dot(a, b, preferred_element_type=jnp.float32)


def each_group(body):
    lax.fori_loop(0, 2, lambda g, _: body(g, pl.multiple_of(HALF * g, TILE)), None)


def kept_lanes(ref, cols, value, keep):
    ref[:, cols] = jnp.where(keep, value, ref[:, cols])


def masked(value, keep):
    return jnp.where(keep, value, jnp.zeros((), value.dtype))


def normalize(s, r):
    x = r["x"][s].reshape(3 * RUN, WIDTH).astype(jnp.float32)
    inverse = lax.rsqrt(jnp.mean(x * x, axis=-1, keepdims=True) + 1e-05)
    r["normed"][...] = (x * inverse * r["scale"][s]).astype(jnp.bfloat16)
    r["inverse"][s] = jnp.broadcast_to(inverse[RUN : 2 * RUN], (RUN, TILE))


def project(s, r, kinds=(0, 1, 2)):
    for t in kinds:
        first = RUN if t == 0 else 0

        def chunk(n, _):
            cols = pl.ds(0, WIDTH)
            r["qkv"][s, t, :, cols] = nn(r["normed"][first : first + 2 * RUN], r["w"][s, t, :, cols]).astype(
                jnp.bfloat16
            )

        chunk(0, None)


def attend(s, r, done):
    att = r["acc"].at[0]

    def group(g, base):
        for j, start, width, offset in windows():
            cols = pl.ds(base + start, width)
            keep = lanes(RUN, width, offset)
            query = masked(r["qkv"][s, 0, :RUN, cols], keep)
            scores = nt(r["qkv"][s, 1, :, cols], query) * (1.0 / math.sqrt(HEAD_DIM)) + r["bias"][...]
            highest = jnp.max(scores, axis=0, keepdims=True)
            exponent = jnp.exp(scores - highest)
            total = jnp.sum(exponent, axis=0, keepdims=True)
            soft = exponent / total
            r["soft"][s, 8 * g + j] = soft
            r["stats"][s, 8 * g + j, :, :RUN] = highest + jnp.log(total)
            kept_lanes(att, cols, tn(soft.astype(jnp.bfloat16), r["qkv"][s, 2, :, cols]), keep)
            if j in (4, 7):
                done(2 * g + j // 7)

    for g in range(2):
        group(g, HALF * g)


def score_grads(s, r):
    def group(g, base):
        for j, start, width, offset in windows():
            cols = pl.ds(base + start, width)
            h = 8 * g + j
            flow = masked(r["flow"][s, 0, :, cols], lanes(RUN, width, offset))
            grad_soft = nt(r["qkv"][s, 2, :, cols], flow)
            soft = r["soft"][s, h]
            inner = jnp.sum(soft * grad_soft, axis=0, keepdims=True)
            r["stats"][2 + s, h, :, :RUN] = inner
            grad = (soft * (grad_soft - inner) * (1.0 / math.sqrt(HEAD_DIM))).astype(jnp.bfloat16)
            r["ds"][h] = grad
            r["softb"][h, :, :RUN] = soft[RUN:].astype(jnp.bfloat16)

    each_group(group)


def query_grads(s, r):
    def group(g, base):
        for j, start, width, offset in windows():
            cols = pl.ds(base + start, width)
            keep = lanes(RUN, width, offset)
            kept_lanes(r["acc"].at[0], cols, tn(r["ds"][8 * g + j], r["qkv"][s, 1, :, cols]), keep)

    each_group(group)
    r["gqkv"][0] = r["acc"][0].astype(jnp.bfloat16)


def next_soft(s, r):
    def group(g, base):
        for j, start, width, offset in windows():
            cols = pl.ds(base + start, width)
            query = masked(r["qkv"][s, 0, RUN:, cols], lanes(RUN, width, offset))
            scores = nt(r["qkv"][s, 1, RUN:, cols], query) * (1.0 / math.sqrt(HEAD_DIM)) + r["bias_next"][...]
            r["soft_next"][8 * g + j] = jnp.exp(scores - r["stats_next"][s, 8 * g + j, :, :RUN])

    each_group(group)


def key_grads(s, r):
    def group(g, base):
        for j, start, width, offset in windows():
            cols = pl.ds(base + start, width)
            h = 8 * g + j
            keep = lanes(RUN, width, offset)
            flow = masked(r["flow"][s, 1, :, cols], keep)
            grad_soft = nt(r["qkv"][s, 2, RUN:, cols], flow)
            soft = r["soft_next"][h]
            grad = (soft * (grad_soft - r["stats_next"][2 + s, h, :, :RUN]) * (1.0 / math.sqrt(HEAD_DIM))).astype(
                jnp.bfloat16
            )
            softb = soft.astype(jnp.bfloat16)
            values = nn(r["softb"][h, :, :RUN], r["flow"][s, 0, :, cols]) + nn(softb, r["flow"][s, 1, :, cols])
            keys = nn(r["ds"][h, RUN:], r["qkv"][s, 0, :RUN, cols]) + nn(grad, r["qkv"][s, 0, RUN:, cols])
            kept_lanes(r["acc"].at[0], cols, keys, keep)
            kept_lanes(r["acc"].at[1], cols, values, keep)

    each_group(group)
    r["gqkv"][1] = r["acc"][0].astype(jnp.bfloat16)
    r["gqkv"][2] = r["acc"][1].astype(jnp.bfloat16)


def back_project(s, r, kinds, add):
    def chunk(n, _):
        rows = pl.ds(0, WIDTH)
        total = nt(r["gqkv"][kinds[0]], r["w"][s, kinds[0], rows, :])
        for t in kinds[1:]:
            total = total + nt(r["gqkv"][t], r["w"][s, t, rows, :])
        if add:
            total = total + r["gn"][:, rows]
        r["gn"][:, rows] = total

    chunk(0, None)


def gain_terms(s, r):
    x = r["x"][s, 1].astype(jnp.float32)
    r["terms"][s : s + 1] = jnp.sum(r["gn"][...] * x * r["inverse"][s][:, :1], axis=0, keepdims=True)


def input_grad(s, r):
    x = r["x"][s, 1].astype(jnp.float32)
    inverse = r["inverse"][s][:, :1]
    grad = r["gn"][...]
    scaled = grad * r["scale"][s]
    moved = inverse * (scaled - x * inverse * inverse * jnp.mean(scaled * x, axis=-1, keepdims=True))
    return (r["flow"][s, 0].astype(jnp.float32) + moved).astype(jnp.bfloat16)


NAMES = (
    "w", "x", "flow", "normed", "inverse", "qkv", "soft", "softb", "soft_next", "ds", "gqkv", "acc", "gn",
    "terms", "stats", "stats_next", "scale", "result", "bias", "bias_next", "raw",
)
SHAPES = [
    pltpu.VMEM((2, 3, WIDTH, WIDTH), jnp.bfloat16),
    pltpu.VMEM((2, 3, RUN, WIDTH), jnp.bfloat16),
    pltpu.VMEM((2, 2, RUN, WIDTH), jnp.bfloat16),
    pltpu.VMEM((3 * RUN, WIDTH), jnp.bfloat16),
    pltpu.VMEM((2, RUN, TILE), jnp.float32),
    pltpu.VMEM((2, 3, 2 * RUN, WIDTH), jnp.bfloat16),
    pltpu.VMEM((2, HEADS, 2 * RUN, RUN), jnp.float32),
    pltpu.VMEM((HEADS, RUN, TILE), jnp.bfloat16),
    pltpu.VMEM((HEADS, RUN, RUN), jnp.float32),
    pltpu.VMEM((HEADS, 2 * RUN, RUN), jnp.bfloat16),
    pltpu.VMEM((3, RUN, WIDTH), jnp.bfloat16),
    pltpu.VMEM((2, RUN, WIDTH), jnp.float32),
    pltpu.VMEM((RUN, WIDTH), jnp.float32),
    pltpu.VMEM((8, WIDTH), jnp.float32),
    pltpu.VMEM((4, HEADS, 1, TILE), jnp.float32),
    pltpu.VMEM((4, HEADS, 1, TILE), jnp.float32),
    pltpu.VMEM((2, 1, WIDTH), jnp.float32),
    pltpu.VMEM((2, RUN, WIDTH), jnp.bfloat16),
    pltpu.VMEM((2 * RUN, RUN), jnp.float32),
    pltpu.VMEM((RUN, RUN), jnp.float32),
    pltpu.VMEM((16, WIDTH), jnp.bfloat16),
]
REDUCE_SCRATCH = [
    pltpu.VMEM((LAYERS, 8, TILE), jnp.float32),
    pltpu.VMEM((LAYERS, 8, TILE), jnp.float32),
    pltpu.VMEM((2, 8, TILE), jnp.float32),
    pltpu.VMEM((2 * PLANE, 8, TILE), jnp.float32),
    pltpu.SemaphoreType.DMA,
    pltpu.SemaphoreType.DMA,
    pltpu.SemaphoreType.DMA,
    pltpu.SemaphoreType.DMA,
]


def whole_kernel(shard, tokens, segments, mask, cotangent, gains, kept_out, got_out, gain_out, *scratch):
    r = dict(zip(NAMES, scratch[: len(NAMES)]))
    hsend, hrecv, local = scratch[len(NAMES) : len(NAMES) + 3]
    rest = scratch[len(NAMES) + 3 :]
    core, dp, z, slot, _, _ = place()
    load = pltpu.make_async_copy(tokens.at[core], r["x"].at[0, 1], local.at[0])
    load.start()
    load_up = pltpu.make_async_copy(cotangent.at[core], r["flow"].at[1, 0], local.at[1])
    load_up.start()
    load_gain = pltpu.make_async_copy(gains, r["scale"].at[core], local.at[2])
    load_gain.start()
    wide = shard[0].astype(jnp.float32)
    parts = [wide[:, WIDTH * t : WIDTH * (t + 1)] for t in range(3)]
    r["raw"][...] = jnp.concatenate(parts + [jnp.zeros((1, WIDTH), jnp.float32)], axis=0).astype(jnp.bfloat16)
    greet(core, dp, z, slot)
    after, before = (dp + 1) % DEVICES, (dp + DEVICES - 1) % DEVICES

    def hand(k, source, target, c, d):
        return pltpu.make_async_remote_copy(
            src_ref=source,
            dst_ref=target,
            send_sem=hsend.at[k],
            recv_sem=hrecv.at[k],
            device_id=(c, d),
            device_id_type=MESH,
        )

    x, flow, stats, stats_next = r["x"], r["flow"], r["stats"], r["stats_next"]
    give_scale = hand(0, gains, r["scale"].at[core], 1 - core, dp)
    give_result = hand(1, r["result"].at[1 - core], got_out, 1 - core, dp)
    give_first = [hand(2, x.at[0, 1], x.at[0, 0], core, after), hand(3, x.at[0, 1], x.at[0, 2], core, before)]
    give_flow = [hand(4 + s, flow.at[s, 0], flow.at[s, 1], core, before) for s in range(2)]
    give_lse = [hand(6 + s, stats.at[s], stats_next.at[s], core, before) for s in range(2)]
    give_inner = [hand(8 + s, stats.at[2 + s], stats_next.at[2 + s], core, before) for s in range(2)]
    give_middle = []
    for p, (start, width) in enumerate(PIECES):
        cols = pl.ds(start, width)
        give_middle.append(hand(10 + 2 * p, x.at[1, 1, :, cols], x.at[1, 0, :, cols], core, after))
        give_middle.append(hand(11 + 2 * p, x.at[1, 1, :, cols], x.at[1, 2, :, cols], core, before))

    def prepare():
        give_scale.start()
        load.wait()
        for h in give_first:
            h.start()
        load_up.wait()
        chosen = down(mask[pl.ds(core, 1), :].astype(jnp.float32)) == 1.0
        flow[1, 0] = jnp.where(chosen, flow[1, 0].astype(jnp.float32), 0.0).astype(jnp.bfloat16)
        give_flow[1].start()
        load_gain.wait()
        fill_biases(segments, r["bias"], r["bias_next"])

    def fill(n):
        if n == 0:
            give_scale.wait_recv()
            for h in give_first:
                h.wait_recv()
            normalize(0, r)
        project(0, r, (n,))

    drain = gather_body(prepare, fill, r["raw"], r["w"], *rest[: len(GATHER_SCRATCH)])
    begin, end = reduce_body(r["terms"], *rest[len(GATHER_SCRATCH) :])

    def middle(g):
        cols = slice(PIECES[g][0], sum(PIECES[g]))
        x[1, 1, :, cols] = (x[0, 1, :, cols].astype(jnp.float32) + r["acc"][0, :, cols]).astype(jnp.bfloat16)
        give_middle[2 * g].start()
        give_middle[2 * g + 1].start()

    attend(0, r, middle)
    give_lse[0].start()
    drain()
    for h in give_middle:
        h.wait_recv()
    normalize(1, r)
    project(1, r)

    def final(g):
        cols = slice(PIECES[g][0], sum(PIECES[g]))
        r["result"][1, :, cols] = (x[1, 1, :, cols].astype(jnp.float32) + r["acc"][0, :, cols]).astype(jnp.bfloat16)

    attend(1, r, final)
    give_lse[1].start()
    give_flow[1].wait_recv()
    for s in (1, 0):
        score_grads(s, r)
        give_inner[s].start()
        query_grads(s, r)
        give_lse[s].wait_recv()
        next_soft(s, r)
        back_project(s, r, (0,), False)
        give_inner[s].wait_recv()
        if s == 0:
            give_flow[0].wait_recv()
        key_grads(s, r)
        back_project(s, r, (1, 2), True)
        gain_terms(s, r)
        if s == 1:
            flow[0, 0] = input_grad(1, r)
            give_flow[0].start()
        else:
            begin()
            r["result"][0] = input_grad(0, r)
    give_result.start()
    keep = pltpu.make_async_copy(r["result"].at[core], kept_out, local.at[3])
    keep.start()
    row, slot = end()
    spread = down(row)
    sub = lax.broadcasted_iota(jnp.int32, (TILE, TILE), 0)
    lane = lax.broadcasted_iota(jnp.int32, (TILE, TILE), 1)
    gain_out[...] = jnp.sum(jnp.where(sub == lane + 5 * slot, spread, 0.0), axis=0, keepdims=True)[:, :5]
    keep.wait()
    give_result.wait_recv()
    for h in [give_scale, give_result] + give_first + give_flow + give_lse + give_inner + give_middle:
        h.wait_send()


def shards(tokens, segment_ids, loss_mask, qkv_weight, gains, cotangent):
    vmem = pl.BlockSpec(memory_space=pltpu.VMEM)
    hbm = pl.BlockSpec(memory_space=pl.ANY)
    kept, got, gain_grad = pl.pallas_call(
        whole_kernel,
        out_shape=(
            jax.ShapeDtypeStruct((RUN, WIDTH), jnp.bfloat16),
            jax.ShapeDtypeStruct((RUN, WIDTH), jnp.bfloat16),
            jax.ShapeDtypeStruct((1, 5), jnp.float32),
        ),
        in_specs=[vmem, hbm, vmem, vmem, hbm, vmem],
        out_specs=(hbm, hbm, vmem),
        scratch_shapes=SHAPES
        + [pltpu.SemaphoreType.DMA((18,)), pltpu.SemaphoreType.DMA((18,)), pltpu.SemaphoreType.DMA((4,))]
        + GATHER_SCRATCH
        + REDUCE_SCRATCH,
        compiler_params=pltpu.CompilerParams(
            collective_id=0, has_side_effects=True, vmem_limit_bytes=56 * 2**20
        ),
        name="sections",
    )(qkv_weight, tokens, segment_ids, loss_mask, cotangent, gains)
    own_first = lax.axis_index("phase") == 0
    pair = [jnp.where(own_first, kept, got), jnp.where(own_first, got, kept)]
    return jnp.stack(pair)[None], gain_grad


def solution(mesh):
    in_specs = (
        P(None, "dp", None),
        P(),
        P(None, "dp"),
        P("phase", "dp", None),
        P("phase", None),
        P(None, "dp", None),
    )
    out_specs = (P("phase", None, "dp", None), P("phase", "dp"))
    return jax.shard_map(shards, mesh=mesh, in_specs=in_specs, out_specs=out_specs, check_vma=False)
```
